128 devices in a mesh: expert: 16 (over y, x), hidden: 8 (over z, core).
Axes of the slice: x: 4, y: 4, z: 4, core: 2. Of those that a mesh axis runs over, the one named last changes fastest.
Arguments:
- tokens: bfloat16 [1024, 7168], P('expert'), may hold values from -6 to 6
- routes: int32 [1024, 8], P('expert'), may hold values from 0 to 31, all different within a row; in each aligned block of 64 rows (0 to 63, 64 to 127, ...) at most 32 rows name the same one
- route_weights: float32 [1024, 8], P('expert'), may hold values from 0.1 to 1
- gate_proj: bfloat16 [32, 7168, 2048], P('expert', None, 'hidden'), may hold values from -0.0625 to 0.0625
- up_proj: bfloat16 [32, 7168, 2048], P('expert', None, 'hidden'), may hold values from -0.0625 to 0.0625
- down_proj: bfloat16 [32, 2048, 7168], P('expert', 'hidden'), may hold values from -0.125 to 0.125
- latents: bfloat16 [1024, 576], P(('expert', 'hidden')), may hold values from -6 to 6
- kv_gain: float32 [512], replicated, may hold values from 0.5 to 1.5
- owners: int32 [1024], P(('expert', 'hidden')), may hold values from 0 to 127, as said below
Outputs:
- moe_out: bfloat16 [1024, 7168], P('expert')
- latent_cache: bfloat16 [2048, 576], P(('expert', 'hidden'))
The draws below stay inside these ranges and needn't reach their ends.
Inputs may be any that keep to these rules, and one draw needn't show every extreme that they name: `routes`: in each aligned block of 64 tokens (the tokens of one index of the expert axis) no expert is named more than 32 times, a bound that some block reaches; the 8 experts of a token differ. Every owner has 1 to 16 tokens; a quarter of the owners have exactly 16, the others fewer.
All inputs are finite; a program needn't handle non-finite values.
Results may differ from the reference program's by a relative error of at most 0.022.
Values may be sent and summed in bfloat16 or wider, within the bound.
A program may use at most 128 MiB of HBM per device.

```python
import math
import jax
import jax.numpy as jnp
import numpy as np
from jax import lax

D = 7168
FFH = 2048
KV_RANK = 512
TOP = 8
TOK_DEV = 64
EXPERTS = 32
CAP = 32
LAT = 576
TOKENS = 1024
SLOTS = 16
N_EXPERT = 16
N_HIDDEN = 8


def draw_owners(key, part):
    key = jax.random.fold_in(key, 7)
    first_key, second_key = jax.random.split(key)
    devices = N_EXPERT * N_HIDDEN
    ranking = jax.random.permutation(first_key, TOKENS).astype(jnp.int32)
    quarter = devices // 4
    half_tokens = TOKENS // 2
    heavy = ranking // SLOTS
    light = quarter + (ranking - half_tokens) % (devices - quarter)
    base = jnp.where(ranking < half_tokens, heavy, light).astype(jnp.int32)
    relabel = jax.random.permutation(second_key, devices).astype(jnp.int32)
    return relabel[base].astype(jnp.int32)


def block_scale(rng, shape, pieces, smallest, largest):
    def one(dim, parts):
        heights = jax.random.uniform(jax.random.fold_in(jax.random.fold_in(rng, 6), dim), (parts,), jnp.float32, smallest / len(pieces), largest / len(pieces))
        return jnp.repeat(jnp.exp(heights), shape[dim] // parts).reshape((-1,) + (1,) * (len(shape) - dim - 1))

    gain = one(*pieces[0])
    for cut in pieces[1:]:
        gain = gain * one(*cut)
    return gain


def deal_out(stream_key, own, number, rows, amount, top, most, skew):
    order = jax.random.permutation(stream_key, amount)
    heavy_load, ordinary = shares(amount, rows * top, most, skew, True), shares(amount, rows * top, most, skew, False)
    places = jnp.arange(amount)

    def named(tallies, offset_by):
        used = int((tallies > 0).sum())
        fixed = max(1, used // 4)
        passed = fixed + (places - fixed + offset_by * (used - fixed)) % max(1, amount - fixed)
        return jnp.zeros((amount,), jnp.int32).at[order[jnp.where(places < fixed, places, passed)]].set(jnp.asarray(tallies, jnp.int32))

    tallies = jnp.where(number % 4 == 0, named(heavy_load, number // 4), named(ordinary, number - number // 4 - 1))
    mixed = jax.random.permutation(jax.random.fold_in(own, 3), amount)
    source_of, taker = mixed[0:amount // 2 * 2:2], mixed[1:amount // 2 * 2:2]
    margin = jnp.minimum(tallies[source_of] - 1, most - tallies[taker]) // 2
    margin = jnp.where((source_of == order[0]) | (taker == order[0]) | (tallies[taker] == 0), 0, jnp.maximum(margin, 0))
    passed = jax.random.randint(jax.random.fold_in(own, 4), (amount // 2,), 0, 1 << 20) % (margin + 1)
    tallies = tallies.at[source_of].add(-passed).at[taker].add(passed)
    members = jnp.searchsorted(jnp.cumsum(tallies), jnp.arange(rows * top), side="right").astype(jnp.int32)
    table = members.reshape(top, rows).T
    table = table[jax.random.permutation(jax.random.fold_in(own, 1), rows)]
    offset_by = jax.random.randint(jax.random.fold_in(own, 2), (rows, 1), 0, top)
    return jnp.take_along_axis(table, (jnp.arange(top)[None, :] + offset_by) % top, axis=1)


def shares(amount, total, reach, skew, full):
    loads = [(1 << 20) // math.isqrt(rank ** skew) + 1 for rank in range(1, amount + 1)]
    largest = reach if full else min(reach, max(-(-total // amount), total * loads[0] // sum(loads)))
    least = 1 if total - largest >= amount - 1 else 0
    given, rest = [largest] + [least] * (amount - 1), total - largest - least * (amount - 1)
    while rest > 0:
        movable = [i for i in range(1, amount) if given[i] < largest] or [i for i in range(1, amount) if given[i] < reach]
        whole, budget = sum([loads[i] for i in movable]), rest
        for i in movable:
            more = min(reach - given[i], max(1, budget * loads[i] // whole), rest)
            given[i] = given[i] + more
            rest = rest - more
    return np.array(given)


def scatter_about(own_key, shape, deviation, reach, shards=(), held_as=jnp.bfloat16):
    values = jax.random.normal(own_key, shape, jnp.float32) * deviation
    if len(shards) > 0:
        values = block_scale(own_key, shape, shards, -0.22, 0.18) * values
    return jnp.clip(values, min=-reach, max=reach).astype(held_as)


def setup_inputs(seed: int = 0) -> dict:
    key_list = jax.random.split(jax.random.key(seed), 10)
    tokens = scatter_about(key_list[0], (TOKENS, D), 1.0, 6.0, ((0, 16),))
    routes_keys = jax.random.split(jax.random.fold_in(key_list[1], 1), TOKENS // TOK_DEV)
    routes_turns = jax.random.permutation(jax.random.fold_in(key_list[1], 3), TOKENS // TOK_DEV)
    routes = jax.vmap(lambda own, number: deal_out(jax.random.fold_in(key_list[1], 2), own, number, TOK_DEV, EXPERTS, TOP, CAP, 2))(routes_keys, routes_turns).reshape((TOKENS, TOP))
    route_weights = jnp.clip(jnp.exp(math.log(1.0) - 2.3025851 * jax.random.uniform(key_list[2], (TOKENS, TOP), jnp.float32) ** block_scale(key_list[2], (TOKENS, TOP), ((0, 16),), -0.2, 0.2)), 0.1, 1.0)
    gate_proj = scatter_about(key_list[3], (EXPERTS, D, FFH), D ** -0.5, 0.0625, ((0, 16), (2, 8)))
    up_proj = scatter_about(key_list[4], (EXPERTS, D, FFH), D ** -0.5, 0.0625, ((0, 16), (2, 8)))
    down_proj = scatter_about(key_list[5], (EXPERTS, FFH, D), FFH ** -0.5, 0.125, ((0, 16), (1, 8)))
    latents = scatter_about(key_list[6], (TOKENS, LAT), 1.0, 6.0, ((0, 128),))
    kv_gain = jnp.clip(1.0 + 0.1 * jax.random.normal(key_list[7], (KV_RANK,), jnp.float32), 0.5, 1.5)
    owners = draw_owners(jax.random.fold_in(key_list[9], 71), 0)
    return dict(tokens=tokens, routes=routes, route_weights=route_weights, gate_proj=gate_proj, up_proj=up_proj, down_proj=down_proj, latents=latents, kv_gain=kv_gain, owners=owners)


def reference(tokens, routes, route_weights, gate_proj, up_proj, down_proj, latents, kv_gain, owners):
    devices = N_EXPERT * N_HIDDEN
    sources = N_EXPERT
    pair_count = TOKENS * TOP
    blocked = routes.reshape(sources, TOK_DEV * TOP)
    expert_ids = jnp.arange(EXPERTS, dtype=jnp.int32)
    onehot = (blocked[:, :, None] == expert_ids[None, None, :]).astype(jnp.int32)
    before = jnp.cumsum(onehot, axis=1) - onehot
    slot_pair = lax.optimization_barrier(jnp.sum(before * onehot, axis=2))
    source_ids = jnp.arange(sources, dtype=jnp.int32)[:, None]
    position = (source_ids * CAP + slot_pair).reshape(-1).astype(jnp.int32)
    pair_expert = routes.reshape(-1).astype(jnp.int32)
    pair_token = (jnp.arange(pair_count, dtype=jnp.int32) // TOP).astype(jnp.int32)
    group_width = FFH // N_HIDDEN

    def one_expert(expert):
        target = jnp.where(pair_expert == expert, position, sources * CAP).astype(jnp.int32)
        token_of = jnp.zeros((sources * CAP,), jnp.int32).at[target].set(pair_token, mode='drop')
        filled = jnp.zeros((sources * CAP,), jnp.int32).at[target].set(1, mode='drop')
        source = tokens[token_of] * filled[:, None].astype(jnp.bfloat16)
        gate_val = jnp.dot(source, gate_proj[expert], preferred_element_type=jnp.float32)
        up_val = jnp.dot(source, up_proj[expert], preferred_element_type=jnp.float32)
        activation = (jax.nn.silu(gate_val) * up_val).astype(jnp.bfloat16)
        act_groups = activation.reshape(sources * CAP, N_HIDDEN, group_width).astype(jnp.float32)
        down_groups = down_proj[expert].reshape(N_HIDDEN, group_width, D).astype(jnp.float32)
        partial_value = jnp.einsum('rgf,gfd->grd', act_groups, down_groups).astype(jnp.bfloat16)
        partial_value = lax.optimization_barrier(partial_value)
        return lax.optimization_barrier(jnp.sum(partial_value.astype(jnp.float32), axis=0)).astype(jnp.bfloat16)
    results = lax.map(one_expert, expert_ids)
    picked = results[pair_expert, position].astype(jnp.float32)
    weighted = picked.reshape(TOKENS, TOP, D) * route_weights[:, :, None]
    moe_out = lax.optimization_barrier(jnp.sum(weighted, axis=1)).astype(jnp.bfloat16)
    wide = latents.astype(jnp.float32)
    head = wide[:, :KV_RANK]
    scale = lax.rsqrt(lax.optimization_barrier(jnp.mean(head * head, axis=1, keepdims=True)) + 1e-06)
    normed = jnp.concatenate([head * scale * kv_gain[None, :], wide[:, KV_RANK:]], axis=1).astype(jnp.bfloat16)
    owner_hot = (owners[:, None] == jnp.arange(devices, dtype=jnp.int32)[None, :]).astype(jnp.int32)
    earlier = lax.optimization_barrier(jnp.sum((jnp.cumsum(owner_hot, axis=0) - owner_hot) * owner_hot, axis=1))
    row_index = (owners * SLOTS + earlier).astype(jnp.int32)
    latent_cache = jnp.zeros((devices * SLOTS, LAT), jnp.bfloat16).at[row_index].set(normed)
    return (moe_out, latent_cache)
```

```python
import functools

import jax
import jax.numpy as jnp
from jax import lax
from jax.experimental import pallas as pl
from jax.experimental.pallas import tpu as pltpu
from jax.sharding import PartitionSpec as P

KV_RANK = 512
TOP = 8
SIDE = 4
ROWS = 64
HALF = 32
QUARTER = 16
WIDE = 7168
PART = 1792
UNITS = 256
N_SEMS = 224
SUBS = ((0, 1024), (1024, 768))

MESH = pl.DeviceIdType.MESH


def moe_kernel(
    tokens,
    routes,
    route_weights,
    gate,
    up,
    down,
    out,
    x,
    w,
    wd,
    acc,
    h,
    gates,
    half_in,
    full_in,
    small_half_in,
    small_full_in,
    own_sum,
    z_in,
    final,
    send_sems,
    recv_sems,
    local_sems,
):
    e = lax.axis_index("expert")
    hid = lax.axis_index("hidden")
    y, xx, z, c = e // SIDE, e % SIDE, hid // 2, hid % 2
    other = 1 - c

    def at(dy=0, dx=0, dz=0, flip=False):
        core = other if flip else c
        return (
            ((y + dy) % SIDE) * SIDE + (xx + dx) % SIDE,
            ((z + dz) % SIDE) * 2 + core,
        )

    x_next, x_prev = at(dx=1), at(dx=3)
    y_next, y_prev = at(dy=1), at(dy=3)
    sibling = at(flip=True)

    keys = {}

    def sem_of(key):
        if key not in keys:
            keys[key] = len(keys)
            assert len(keys) <= N_SEMS
        return keys[key]

    pending = []

    def send(key, src, dst, device):
        i = sem_of(key)
        copy = pltpu.make_async_remote_copy(
            src_ref=src,
            dst_ref=dst,
            send_sem=send_sems.at[i],
            recv_sem=recv_sems.at[i],
            device_id=device,
            device_id_type=MESH,
        )
        copy.start()
        pending.append(copy)

    def arrived(key, landing):
        i = sem_of(key)
        pltpu.make_async_remote_copy(
            src_ref=landing,
            dst_ref=landing,
            send_sem=send_sems.at[i],
            recv_sem=recv_sems.at[i],
            device_id=sibling,
            device_id_type=MESH,
        ).wait_recv()

    def settle():
        for copy in pending:
            copy.wait_send()
        pending.clear()

    locals_ = []

    def local(src, dst):
        copy = pltpu.make_async_copy(src, dst, local_sems.at[len(locals_)])
        copy.start()
        locals_.append(copy)
        return copy

    big = (y, xx)
    small = (xx, y)
    big_next, big_prev = (y_next, x_next), (y_prev, x_prev)
    small_next, small_prev = (x_next, y_next), (x_prev, y_prev)
    STEP = (0, 3, 1, 2)

    def big_at(k, q):
        return (big[k] + STEP[q]) % SIDE

    def small_at(k, r):
        return (small[k] + STEP[r]) % SIDE

    def token_columns(k, half):
        return pl.ds(pl.multiple_of(half * (2 * PART) + k * PART, 128), PART)

    LOW, HIGH = pl.ds(0, HALF), pl.ds(HALF, HALF)
    GLOW, GHIGH = pl.ds(0, HALF // 2), pl.ds(HALF // 2, HALF // 2)

    weight_loads = [local(gate, w.at[pl.ds(0, 2)]), local(up, w.at[pl.ds(2, 2)])]
    token_loads = [
        local(tokens.at[:, token_columns(k, half)], x.at[k, half, big[k], small[k]])
        for k in range(2)
        for half in range(2)
    ]

    chosen = routes[...]
    strength = route_weights[...]
    lanes = lax.broadcasted_iota(jnp.int32, (ROWS, 128), 1)
    dense = jnp.zeros((ROWS, 128), jnp.float32)
    for j in range(TOP):
        dense = dense + jnp.where(lanes % 32 == chosen[:, j : j + 1], strength[:, j : j + 1], 0.0)
    dense_high = dense.astype(jnp.bfloat16).astype(jnp.float32)
    mixed = jnp.where(lanes % 64 < 32, dense_high, dense - dense_high)
    packed = jnp.where(lanes[:HALF] < 64, mixed[:HALF], mixed[HALF:])
    gates[y, xx] = packed.astype(jnp.bfloat16)
    acc[...] = jnp.zeros_like(acc)

    barrier = pltpu.get_barrier_semaphore()
    partners = (x_next, x_prev, y_next, y_prev, at(dz=1), at(dz=2), at(dz=3), sibling)
    for partner in partners:
        pl.semaphore_signal(barrier, inc=1, device_id=partner, device_id_type=MESH)
    pl.semaphore_wait(barrier, len(partners))

    def block(k, q, r):
        return x.at[k, c, big_at(k, q), small_at(k, r)]

    def gate_block(q, r):
        return gates.at[big_at(0, q), small_at(0, r)]

    def send_block(key, k, q, r, device, rows=None):
        ref = block(k, q, r)
        if rows is not None:
            ref = ref.at[rows]
        send(key, ref, ref, device)
        if k == 0:
            ref = gate_block(q, r)
            if rows is not None:
                ref = ref.at[GLOW if rows is LOW else GHIGH]
            send(("g",) + key, ref, ref, device)

    def block_arrived(key, k, q, r, rows=None):
        ref = block(k, q, r)
        if rows is not None:
            ref = ref.at[rows]
        arrived(key, ref)
        if k == 0:
            ref = gate_block(q, r)
            if rows is not None:
                ref = ref.at[GLOW if rows is LOW else GHIGH]
            arrived(("g",) + key, ref)

    def send_own(key, k, device):
        send(key, tokens.at[:, token_columns(k, c)], block(k, 0, 0), device)
        if k == 0:
            send(("g",) + key, gate_block(0, 0), gate_block(0, 0), device)

    def to_sibling(k, q, r):
        send(("c", k, q, r), block(k, q, r), block(k, q, r), sibling)

    def from_sibling(k, q, r):
        arrived(("c", k, q, r), x.at[k, other, big_at(k, q), small_at(k, r)])

    for k in (1, 0):
        send_own(("s1p", k), k, small_next[k])
        send_own(("s1m", k), k, small_prev[k])
    for k in (0, 1):
        send_own(("b1p", k, 0), k, big_next[k])
        send_own(("b1m", k, 0), k, big_prev[k])
    down_half = pl.ds(pl.multiple_of(c * (2 * PART), 128), 2 * PART)
    down_other = pl.ds(pl.multiple_of(other * (2 * PART), 128), 2 * PART)
    send(("wd",), down.at[:, :, down_other], wd.at[c], sibling)
    down_load = local(down.at[:, :, down_half], wd.at[c])

    for k in (0, 1):
        block_arrived(("s1p", k), k, 0, 1)
        send_block(("s2p", k), k, 0, 1, small_next[k], LOW)
        block_arrived(("s1m", k), k, 0, 2)
        send_block(("s2m", k), k, 0, 2, small_prev[k], HIGH)
    for r in (1, 2):
        for k in (0, 1):
            send_block(("b1p", k, r), k, 0, r, big_next[k])
            send_block(("b1m", k, r), k, 0, r, big_prev[k])
            to_sibling(k, 0, r)
    for k in (0, 1):
        block_arrived(("s2p", k), k, 0, 3, LOW)
        block_arrived(("s2m", k), k, 0, 3, HIGH)
        send_block(("b1p", k, 3), k, 0, 3, big_next[k])
        send_block(("b1m", k, 3), k, 0, 3, big_prev[k])
        to_sibling(k, 0, 3)

    def long_step(r):
        for k in (0, 1):
            block_arrived(("b1p", k, r), k, 1, r)
            send_block(("b2p", k, r), k, 1, r, big_next[k], LOW)
            block_arrived(("b1m", k, r), k, 2, r)
            send_block(("b2m", k, r), k, 2, r, big_prev[k], HIGH)
            to_sibling(k, 1, r)
            to_sibling(k, 2, r)

    def far_step(r):
        for k in (0, 1):
            block_arrived(("b2p", k, r), k, 3, r, LOW)
            block_arrived(("b2m", k, r), k, 3, r, HIGH)
            to_sibling(k, 3, r)

    def multiply(k, half, q):
        g = big_at(k, q)
        start = half * (2 * PART) + k * PART

        def one(n, carry):
            left = x[k, half, g].reshape(SIDE * ROWS, PART)
            right = w[n, pl.ds(pl.multiple_of(start, 128), PART), :]
            part = jnp.dot(left, right, preferred_element_type=jnp.float32)
            part = part.reshape(SIDE, ROWS, UNITS)
            if k == 0:
                acc[n, g] += part
            else:
                acc[n, :, g] += part
            return carry

        lax.fori_loop(0, 4, one, 0)

    for copy in weight_loads + token_loads:
        copy.wait()
    long_step(0)
    for k in (0, 1):
        multiply(k, c, 0)
    long_step(1)
    for k in (0, 1):
        for r in (1, 2, 3):
            from_sibling(k, 0, r)
        multiply(k, other, 0)
    long_step(2)
    long_step(3)
    for q in (1, 2):
        for k in (0, 1):
            multiply(k, c, q)
            if q == 1:
                far_step(k)
    for q in (1, 2):
        for k in (0, 1):
            for r in range(SIDE):
                from_sibling(k, q, r)
            multiply(k, other, q)
            if q == 1:
                far_step(2 + k)
    for k in (0, 1):
        multiply(k, c, 3)
    for k in (0, 1):
        for r in range(SIDE):
            from_sibling(k, 3, r)
        multiply(k, other, 3)

    lane = lax.broadcasted_iota(jnp.int32, (128, 2 * UNITS), 0)
    column = lax.broadcasted_iota(jnp.int32, (128, 2 * UNITS), 1)
    wanted = (lane % 32) == (2 * e + column // UNITS)
    pick_low = (wanted & (lane < 64)).astype(jnp.bfloat16)
    pick_high = (wanted & (lane >= 64)).astype(jnp.bfloat16)
    own_units = pl.ds(pl.multiple_of(c * (2 * UNITS), 128), 2 * UNITS)
    other_units = pl.ds(pl.multiple_of(other * (2 * UNITS), 128), 2 * UNITS)

    def activate(q):
        g = big_at(0, q)
        packed_rows = gates[g].reshape(SIDE * HALF, 128)
        low = jnp.dot(packed_rows, pick_low, preferred_element_type=jnp.float32)
        high = jnp.dot(packed_rows, pick_high, preferred_element_type=jnp.float32)
        weight = jnp.concatenate(
            [
                low.reshape(SIDE, HALF, 2 * UNITS),
                high.reshape(SIDE, HALF, 2 * UNITS),
            ],
            axis=1,
        )
        for n in range(2):
            gate_val = acc[n, g]
            value = gate_val / (1.0 + jnp.exp(-gate_val)) * acc[2 + n, g]
            value = value * weight[:, :, n * UNITS : (n + 1) * UNITS]
            where = pl.ds(pl.multiple_of(c * (2 * UNITS) + n * UNITS, 128), UNITS)
            h[g, :, :, where] = value.astype(jnp.bfloat16)
        send(("h", q), h.at[g, :, :, own_units], h.at[g, :, :, own_units], sibling)

    for q in (3, 1, 2, 0):
        activate(q)
    settle()
    down_load.wait()
    arrived(("wd",), wd.at[other])
    for q in (3, 1, 2, 0):
        arrived(("h", q), h.at[big_at(0, q), :, :, other_units])

    FAR, NEXT, PREV, MINE = 0, 1, 2, 3

    def stage(k, slot):
        return x.at[k, 0, slot]

    def partial(k, q, s, slot, add):
        g = big_at(k, q)
        first, width = SUBS[s]

        def one(n, carry):
            start = pl.multiple_of(first + n * 256, 128)
            cols = pl.ds(start, 256)
            left = h[g] if k == 0 else h[:, g]
            right = wd[:, :, :, pl.ds(pl.multiple_of(k * PART + start, 128), 256)]
            part = jnp.dot(
                left.reshape(SIDE * ROWS, 4 * UNITS),
                right.reshape(4 * UNITS, 256),
                preferred_element_type=jnp.float32,
            ).reshape(SIDE, ROWS, 256)
            if add == "low":
                x[k, 0, slot, :, LOW, cols] = (
                    part[:, :HALF] + half_in[k, 0, :, :, cols].astype(jnp.float32)
                ).astype(jnp.bfloat16)
                x[k, 0, slot, :, HIGH, cols] = part[:, HALF:].astype(jnp.bfloat16)
            elif add == "high":
                x[k, 0, slot, :, LOW, cols] = part[:, :HALF].astype(jnp.bfloat16)
                x[k, 0, slot, :, HIGH, cols] = (
                    part[:, HALF:] + half_in[k, 1, :, :, cols].astype(jnp.float32)
                ).astype(jnp.bfloat16)
            else:
                if add == "both":
                    part = part + full_in[k, 0, :, :, cols].astype(jnp.float32)
                    part = part + full_in[k, 1, :, :, cols].astype(jnp.float32)
                x[k, 0, slot, :, :, cols] = part.astype(jnp.bfloat16)
            return carry

        lax.fori_loop(0, width // 256, one, 0)

    def piece(s):
        return pl.ds(*SUBS[s])

    def back_far(k, s):
        partial(k, 3, s, FAR, None)
        cols = piece(s)
        send(
            ("rhp", k, s),
            stage(k, FAR).at[:, LOW, cols],
            half_in.at[k, 0, :, :, cols],
            big_next[k],
        )
        send(
            ("rhm", k, s),
            stage(k, FAR).at[:, HIGH, cols],
            half_in.at[k, 1, :, :, cols],
            big_prev[k],
        )

    def back_near(k, s):
        cols = piece(s)
        arrived(("rhp", k, s), half_in.at[k, 0, :, :, cols])
        partial(k, 2, s, NEXT, "low")
        send(("rfp", k, s), stage(k, NEXT).at[:, :, cols], full_in.at[k, 0, :, :, cols], big_next[k])
        arrived(("rhm", k, s), half_in.at[k, 1, :, :, cols])
        partial(k, 1, s, PREV, "high")
        send(("rfm", k, s), stage(k, PREV).at[:, :, cols], full_in.at[k, 1, :, :, cols], big_prev[k])

    def back_mine(k, s):
        cols = piece(s)
        arrived(("rfp", k, s), full_in.at[k, 0, :, :, cols])
        arrived(("rfm", k, s), full_in.at[k, 1, :, :, cols])
        partial(k, 0, s, MINE, "both")
        far = stage(k, MINE).at[small_at(k, 3)]
        send(("thp", k, s), far.at[LOW, cols], small_half_in.at[k, 0, :, cols], small_next[k])
        send(("thm", k, s), far.at[HIGH, cols], small_half_in.at[k, 1, :, cols], small_prev[k])

    def back_small(k, s):
        cols = piece(s)
        arrived(("thp", k, s), small_half_in.at[k, 0, :, cols])
        j = small_at(k, 2)
        x[k, 0, MINE, j, LOW, cols] = (
            x[k, 0, MINE, j, LOW, cols].astype(jnp.float32)
            + small_half_in[k, 0, :, cols].astype(jnp.float32)
        ).astype(jnp.bfloat16)
        send(("tfp", k, s), stage(k, MINE).at[j, :, cols], small_full_in.at[k, 0, :, cols], small_next[k])
        arrived(("thm", k, s), small_half_in.at[k, 1, :, cols])
        j = small_at(k, 1)
        x[k, 0, MINE, j, HIGH, cols] = (
            x[k, 0, MINE, j, HIGH, cols].astype(jnp.float32)
            + small_half_in[k, 1, :, cols].astype(jnp.float32)
        ).astype(jnp.bfloat16)
        send(("tfm", k, s), stage(k, MINE).at[j, :, cols], small_full_in.at[k, 1, :, cols], small_prev[k])

    def z_rows(d):
        return pl.ds(pl.multiple_of(((z + d) % SIDE) * QUARTER, QUARTER), QUARTER)

    def back_block(k, s):
        cols = piece(s)
        arrived(("tfp", k, s), small_full_in.at[k, 0, :, cols])
        arrived(("tfm", k, s), small_full_in.at[k, 1, :, cols])
        own_sum[k, :, cols] = (
            x[k, 0, MINE, small[k], :, cols].astype(jnp.float32)
            + small_full_in[k, 0, :, cols].astype(jnp.float32)
            + small_full_in[k, 1, :, cols].astype(jnp.float32)
        ).astype(jnp.bfloat16)
        for d in (2, 1, 3):
            send(
                ("z", k, s, d),
                own_sum.at[k, z_rows(d), cols],
                z_in.at[k, d - 1, :, cols],
                at(dz=d),
            )

    def back_z(k, s):
        cols = piece(s)
        for d in (1, 2, 3):
            arrived(("z", k, s, d), z_in.at[k, d - 1, :, cols])
        total = own_sum[k, z_rows(0), cols].astype(jnp.float32)
        for d in (1, 2, 3):
            total = total + z_in[k, d - 1, :, cols].astype(jnp.float32)
        final[k, z_rows(0), cols] = total.astype(jnp.bfloat16)
        for d in (2, 1, 3):
            mine = final.at[k, z_rows(0), cols]
            send(("f", k, s, d), mine, mine, at(dz=d))

    last = []

    def back_out(k, s):
        cols = piece(s)
        for d in (1, 2, 3):
            arrived(("f", k, s, d), final.at[k, z_rows(SIDE - d), cols])
        first, width = SUBS[s]
        where = pl.ds(pl.multiple_of(c * (2 * PART) + k * PART + first, 128), width)
        send(("o", k, s), final.at[k, :, cols], out.at[:, where], sibling)
        last.append(local(final.at[k, :, cols], out.at[:, where]))

    def back_sibling(k, s):
        first, width = SUBS[s]
        where = pl.ds(pl.multiple_of(other * (2 * PART) + k * PART + first, 128), width)
        arrived(("o", k, s), out.at[:, where])

    both = (0, 1)
    for s in both:
        for k in both:
            back_far(k, s)
    for s in both:
        for k in both:
            back_near(k, s)
    for k in both:
        back_mine(k, 0)
    for k in both:
        back_small(k, 0)
    for k in both:
        back_block(k, 0)
    for k in both:
        back_z(k, 0)
    for k in both:
        back_mine(k, 1)
    for k in both:
        back_small(k, 1)
    for k in both:
        back_block(k, 1)
    for k in both:
        back_out(k, 0)
    for k in both:
        back_z(k, 1)
    for k in both:
        back_out(k, 1)
    for s in both:
        for k in both:
            back_sibling(k, s)
    for copy in last:
        copy.wait()
    settle()


def moe(tokens, routes, route_weights, gate, up, down):
    bf16 = jnp.bfloat16
    anywhere = pl.BlockSpec(memory_space=pl.ANY)
    vmem = pl.BlockSpec(memory_space=pltpu.VMEM)
    return pl.pallas_call(
        moe_kernel,
        out_shape=jax.ShapeDtypeStruct((ROWS, WIDE), bf16),
        in_specs=[anywhere, vmem, vmem, anywhere, anywhere, anywhere],
        out_specs=anywhere,
        scratch_shapes=[
            pltpu.VMEM((2, 2, SIDE, SIDE, ROWS, PART), bf16),
            pltpu.VMEM((4, WIDE, UNITS), bf16),
            pltpu.VMEM((2, 2, UNITS, 2 * PART), bf16),
            pltpu.VMEM((4, SIDE, SIDE, ROWS, UNITS), jnp.float32),
            pltpu.VMEM((SIDE, SIDE, ROWS, 4 * UNITS), bf16),
            pltpu.VMEM((SIDE, SIDE, HALF, 128), bf16),
            pltpu.VMEM((2, 2, SIDE, HALF, PART), bf16),
            pltpu.VMEM((2, 2, SIDE, ROWS, PART), bf16),
            pltpu.VMEM((2, 2, HALF, PART), bf16),
            pltpu.VMEM((2, 2, ROWS, PART), bf16),
            pltpu.VMEM((2, ROWS, PART), bf16),
            pltpu.VMEM((2, 3, QUARTER, PART), bf16),
            pltpu.VMEM((2, ROWS, PART), bf16),
            pltpu.SemaphoreType.DMA((N_SEMS,)),
            pltpu.SemaphoreType.DMA((N_SEMS,)),
            pltpu.SemaphoreType.DMA((16,)),
        ],
        compiler_params=pltpu.CompilerParams(
            collective_id=0, has_side_effects=True, vmem_limit_bytes=60 << 20
        ),
        cost_estimate=pl.CostEstimate(
            flops=2 * 3 * 1024 * WIDE * 512, bytes_accessed=24 << 20, transcendentals=1 << 19
        ),
        name="moe",
    )(tokens, routes, route_weights, gate, up, down)


def body(tokens, routes, route_weights, gate_proj, up_proj, down_proj, latents, kv_gain, owners):
    n_hidden = lax.axis_size("hidden")
    wide = latents.astype(jnp.float32)
    head_part = wide[:, :KV_RANK]
    scale = lax.rsqrt(jnp.mean(head_part * head_part, axis=1, keepdims=True) + 1e-06)
    marks = jnp.broadcast_to(owners.astype(jnp.float32)[:, None], (owners.shape[0], 64))
    normed = jnp.concatenate(
        [head_part * scale * kv_gain[None, :], wide[:, KV_RANK:], marks], axis=1
    ).astype(jnp.bfloat16)
    all_latent = lax.all_gather(normed, ("expert", "hidden"), axis=0, tiled=True)

    moe_out = moe(tokens, routes, route_weights, gate_proj, up_proj, down_proj)

    my_index = lax.axis_index("expert") * n_hidden + lax.axis_index("hidden")
    cache_rows = 2 * latents.shape[0]
    slot_ids = jnp.arange(cache_rows, dtype=jnp.int32)[:, None]
    all_owner = all_latent[:, latents.shape[1]].astype(jnp.int32)
    mine = (all_owner == my_index).astype(jnp.int32)
    earlier = jnp.cumsum(mine) - mine
    placing = ((earlier[None, :] == slot_ids) & (mine[None, :] == 1)).astype(jnp.bfloat16)
    latent_cache = jnp.dot(
        placing, all_latent[:, : latents.shape[1]], preferred_element_type=jnp.float32
    ).astype(jnp.bfloat16)
    return (moe_out, latent_cache)


def solution(mesh):
    return jax.shard_map(
        body,
        mesh=mesh,
        in_specs=(
            P("expert", None),
            P("expert", None),
            P("expert", None),
            P("expert", None, "hidden"),
            P("expert", None, "hidden"),
            P("expert", "hidden", None),
            P(("expert", "hidden"), None),
            P(),
            P(("expert", "hidden")),
        ),
        out_specs=(P("expert", None), P(("expert", "hidden"), None)),
        check_vma=False,
    )
```

```python
import functools

import jax
import jax.numpy as jnp
from jax import lax
from jax.experimental import pallas as pl
from jax.experimental.pallas import tpu as pltpu
from jax.sharding import PartitionSpec as P

KV_RANK = 512
LAT = 576
LAT_PART = 384
LAT_COLS = pl.ds(0, LAT_PART)
SIDE_COLS = 512
SLOTS = 16
N_EXPERTS = 32
TOP = 8
SIDE = 4
ROWS = 64
HALF = 32
QUARTER = 16
WIDE = 7168
PART = 1792
UNITS = 256
N_SEMS = 256
SUBS = ((0, 768), (768, 512))
FIRST = 1280
OWN = 128

MESH = pl.DeviceIdType.MESH


def moe_kernel(
    tokens,
    routes,
    route_weights,
    gate,
    up,
    down,
    latents,
    kv_gain,
    owners,
    out,
    cache,
    x,
    w,
    wd,
    acc,
    h,
    normed,
    side,
    lat,
    z_first_in,
    half_in,
    full_in,
    small_half_in,
    small_full_in,
    own_sum,
    z_in,
    final,
    send_sems,
    recv_sems,
    local_sems,
):
    e = lax.axis_index("expert")
    hid = lax.axis_index("hidden")
    y, xx, z, c = e // SIDE, e % SIDE, hid // 2, hid % 2
    other = 1 - c

    def at(dy=0, dx=0, dz=0, flip=False):
        core = other if flip else c
        return (
            ((y + dy) % SIDE) * SIDE + (xx + dx) % SIDE,
            ((z + dz) % SIDE) * 2 + core,
        )

    x_next, x_prev = at(dx=1), at(dx=3)
    y_next, y_prev = at(dy=1), at(dy=3)
    sibling = at(flip=True)

    keys = {}

    def sem_of(key):
        if key not in keys:
            keys[key] = len(keys)
            assert len(keys) <= N_SEMS
        return keys[key]

    pending = []

    def send(key, src, dst, device):
        i = sem_of(key)
        copy = pltpu.make_async_remote_copy(
            src_ref=src,
            dst_ref=dst,
            send_sem=send_sems.at[i],
            recv_sem=recv_sems.at[i],
            device_id=device,
            device_id_type=MESH,
        )
        copy.start()
        pending.append(copy)

    def arrived(key, landing):
        i = sem_of(key)
        pltpu.make_async_remote_copy(
            src_ref=landing,
            dst_ref=landing,
            send_sem=send_sems.at[i],
            recv_sem=recv_sems.at[i],
            device_id=sibling,
            device_id_type=MESH,
        ).wait_recv()

    def settle():
        for copy in pending:
            copy.wait_send()
        pending.clear()

    locals_ = []

    def local(src, dst):
        copy = pltpu.make_async_copy(src, dst, local_sems.at[len(locals_)])
        copy.start()
        locals_.append(copy)
        return copy

    big = (y, xx)
    small = (xx, y)
    big_next, big_prev = (y_next, x_next), (y_prev, x_prev)
    small_next, small_prev = (x_next, y_next), (x_prev, y_prev)
    STEP = (0, 3, 1, 2)

    def big_at(k, q):
        return (big[k] + STEP[q]) % SIDE

    def small_at(k, r):
        return (small[k] + STEP[r]) % SIDE

    def token_columns(k, half):
        return pl.ds(pl.multiple_of(half * (2 * PART) + k * PART, 128), PART)

    LOW, HIGH = pl.ds(0, HALF), pl.ds(HALF, HALF)

    weight_loads = [local(gate, w.at[pl.ds(0, 2)]), local(up, w.at[pl.ds(2, 2)])]
    token_loads = [
        local(tokens.at[:, token_columns(k, half)], x.at[k, half, big[k], small[k]])
        for k in range(2)
        for half in range(2)
    ]

    chosen = routes[...]
    strength = route_weights[...]
    expert_row = lax.broadcasted_iota(jnp.int32, (N_EXPERTS, ROWS), 0)
    dense = jnp.zeros((N_EXPERTS, ROWS), jnp.float32)
    for j in range(TOP):
        dense = dense + jnp.where(expert_row == chosen[j : j + 1], strength[j : j + 1], 0.0)
    dense_high = dense.astype(jnp.bfloat16).astype(jnp.float32)
    packed = jnp.concatenate([dense_high, dense - dense_high], axis=1)
    packed = jnp.where(c == 0, packed[:QUARTER], packed[QUARTER:])

    head = latents[:, :KV_RANK].astype(jnp.float32)
    tail = latents[:, KV_RANK:].astype(jnp.float32)
    scale = lax.rsqrt(jnp.sum(head * head, axis=1, keepdims=True) / KV_RANK + 1e-06)
    lat_rows = latents.shape[0]
    row = lax.broadcasted_iota(jnp.int32, (lat_rows, 2 * LAT_PART - LAT), 0)
    marks = jnp.zeros(row.shape, jnp.float32)
    for i in range(lat_rows):
        marks = jnp.where(row == i, owners[i].astype(jnp.float32), marks)
    normed[0, :, :KV_RANK] = head * scale * kv_gain[...]
    normed[0, :, KV_RANK:] = jnp.concatenate([tail, marks], axis=1)
    acc[...] = jnp.zeros_like(acc)

    barrier = pltpu.get_barrier_semaphore()
    partners = (x_next, x_prev, y_next, y_prev, at(dz=1), at(dz=2), at(dz=3), sibling)
    for partner in partners:
        pl.semaphore_signal(barrier, inc=1, device_id=partner, device_id_type=MESH)
    pl.semaphore_wait(barrier, len(partners))

    def block(k, q, r):
        return x.at[k, c, big_at(k, q), small_at(k, r)]

    def send_block(key, k, q, r, device, rows=None):
        ref = block(k, q, r)
        if rows is not None:
            ref = ref.at[rows]
        send(key, ref, ref, device)

    def block_arrived(key, k, q, r, rows=None):
        ref = block(k, q, r)
        if rows is not None:
            ref = ref.at[rows]
        arrived(key, ref)

    def send_own(key, k, device):
        send(key, tokens.at[:, token_columns(k, c)], block(k, 0, 0), device)

    SIDE_LEFT, SIDE_RIGHT = pl.ds(0, SIDE_COLS // 2), pl.ds(SIDE_COLS // 2, SIDE_COLS // 2)

    def side_ref(dy=0, dx=0):
        return side.at[c, (y + dy) % SIDE, (xx + dx) % SIDE]

    def side_row(dy=0):
        return side.at[c, (y + dy) % SIDE]

    def side_one():
        arrived(("n",), normed.at[1])
        first = jnp.where(c == 0, normed[0], normed[1])
        second = jnp.where(c == 0, normed[1], normed[0])
        pair = jnp.concatenate([first, second], axis=0)
        pair = jnp.where(c == 0, pair[:, :LAT_PART], pair[:, LAT_PART:])
        side[c, y, xx] = jnp.concatenate([pair, packed], axis=1).astype(jnp.bfloat16)
        send(("g1p",), side_ref(), side_ref(), x_next)
        send(("g1m",), side_ref(), side_ref(), x_prev)

    def side_two():
        arrived(("g1p",), side_ref(dx=3))
        ref = side_ref(dx=3).at[:, SIDE_LEFT]
        send(("g2p",), ref, ref, x_next)
        arrived(("g1m",), side_ref(dx=1))
        ref = side_ref(dx=1).at[:, SIDE_RIGHT]
        send(("g2m",), ref, ref, x_prev)

    def side_three():
        arrived(("g2p",), side_ref(dx=2).at[:, SIDE_LEFT])
        arrived(("g2m",), side_ref(dx=2).at[:, SIDE_RIGHT])
        send(("g3p",), side_row(), side_row(), y_next)
        send(("g3m",), side_row(), side_row(), y_prev)

    def side_four():
        arrived(("g3p",), side_row(3))
        ref = side_row(3).at[:, :, SIDE_LEFT]
        send(("g4p",), ref, ref, y_next)
        arrived(("g3m",), side_row(1))
        ref = side_row(1).at[:, :, SIDE_RIGHT]
        send(("g4m",), ref, ref, y_prev)

    def side_done():
        arrived(("g4p",), side_row(2).at[:, :, SIDE_LEFT])
        arrived(("g4m",), side_row(2).at[:, :, SIDE_RIGHT])
        send(("gc",), side.at[c], side.at[c], sibling)
        for d in (2, 1, 3):
            send(("lz", d), side.at[c, :, :, :, LAT_COLS], lat.at[c, :, :, z], at(dz=d))

    def to_sibling(k, q, r):
        send(("c", k, q, r), block(k, q, r), block(k, q, r), sibling)

    def from_sibling(k, q, r):
        arrived(("c", k, q, r), x.at[k, other, big_at(k, q), small_at(k, r)])

    send(("n",), normed.at[0], normed.at[1], sibling)
    for k in (1, 0):
        send_own(("s1p", k), k, small_next[k])
        send_own(("s1m", k), k, small_prev[k])
    for k in (0, 1):
        send_own(("b1p", k, 0), k, big_next[k])
        send_own(("b1m", k, 0), k, big_prev[k])
    side_one()
    down_half = pl.ds(pl.multiple_of(c * (2 * PART), 128), 2 * PART)
    down_other = pl.ds(pl.multiple_of(other * (2 * PART), 128), 2 * PART)
    send(("wd",), down.at[:, :, down_other], wd.at[c], sibling)
    down_load = local(down.at[:, :, down_half], wd.at[c])

    for k in (0, 1):
        block_arrived(("s1p", k), k, 0, 1)
        send_block(("s2p", k), k, 0, 1, small_next[k], LOW)
        block_arrived(("s1m", k), k, 0, 2)
        send_block(("s2m", k), k, 0, 2, small_prev[k], HIGH)
    for r in (1, 2):
        for k in (0, 1):
            send_block(("b1p", k, r), k, 0, r, big_next[k])
            send_block(("b1m", k, r), k, 0, r, big_prev[k])
            to_sibling(k, 0, r)
    for k in (0, 1):
        block_arrived(("s2p", k), k, 0, 3, LOW)
        block_arrived(("s2m", k), k, 0, 3, HIGH)
        send_block(("b1p", k, 3), k, 0, 3, big_next[k])
        send_block(("b1m", k, 3), k, 0, 3, big_prev[k])
        to_sibling(k, 0, 3)
    side_two()

    def long_step(r):
        for k in (0, 1):
            block_arrived(("b1p", k, r), k, 1, r)
            send_block(("b2p", k, r), k, 1, r, big_next[k], LOW)
            block_arrived(("b1m", k, r), k, 2, r)
            send_block(("b2m", k, r), k, 2, r, big_prev[k], HIGH)
            to_sibling(k, 1, r)
            to_sibling(k, 2, r)

    def far_step(r):
        for k in (0, 1):
            block_arrived(("b2p", k, r), k, 3, r, LOW)
            block_arrived(("b2m", k, r), k, 3, r, HIGH)
            to_sibling(k, 3, r)

    def multiply(k, half, blocks):
        start = half * (2 * PART) + k * PART
        places = [(big_at(k, q), small_at(k, r)) for q, r in blocks]

        def one(n, carry):
            left = jnp.concatenate([x[k, half, g, j] for g, j in places], axis=0)
            right = w[n, pl.ds(pl.multiple_of(start, 128), PART), :]
            part = jnp.dot(left, right, preferred_element_type=jnp.float32)
            for i, (g, j) in enumerate(places):
                piece = part[i * ROWS : (i + 1) * ROWS]
                if k == 0:
                    acc[n, g, j] += piece
                else:
                    acc[n, j, g] += piece
            return carry

        lax.fori_loop(0, 4, one, 0)

    NEAR_ROW = ((0, 0), (0, 1), (0, 2), (0, 3))
    EARLY = ((1, 0), (1, 1), (2, 0), (2, 1))
    LATE = ((1, 2), (1, 3), (2, 2), (2, 3))
    FAR_ROW = ((3, 0), (3, 1), (3, 2), (3, 3))

    def rest(k, blocks):
        for q, r in blocks:
            if (q, r) != (0, 0):
                from_sibling(k, q, r)
        multiply(k, other, blocks)

    for copy in weight_loads + token_loads:
        copy.wait()
    long_step(0)
    for k in (0, 1):
        multiply(k, c, NEAR_ROW)
    side_three()
    long_step(1)
    for k in (0, 1):
        rest(k, NEAR_ROW)
    for k in (0, 1):
        multiply(k, c, EARLY)
    long_step(2)
    for k in (0, 1):
        rest(k, EARLY)
    side_four()
    long_step(3)
    far_step(0)
    for k in (0, 1):
        multiply(k, c, LATE)
    far_step(1)
    for k in (0, 1):
        rest(k, LATE)
    side_done()
    far_step(2)
    far_step(3)
    for k in (0, 1):
        multiply(k, c, FAR_ROW)
    for k in (0, 1):
        rest(k, FAR_ROW)

    expert = lax.broadcasted_iota(jnp.int32, (N_EXPERTS, 2 * UNITS), 0)
    column = lax.broadcasted_iota(jnp.int32, (N_EXPERTS, 2 * UNITS), 1)
    pick = (expert == 2 * e + column // UNITS).astype(jnp.bfloat16)
    arrived(("gc",), side.at[other])
    own_units = pl.ds(pl.multiple_of(c * (2 * UNITS), 128), 2 * UNITS)
    other_units = pl.ds(pl.multiple_of(other * (2 * UNITS), 128), 2 * UNITS)

    def activate(q):
        g = big_at(0, q)
        weights = []
        for j in range(SIDE):
            halves = [side[core, g, j, :, 3 * 128 :] for core in range(2)]
            both_parts = lax.dot_general(
                jnp.concatenate(halves, axis=0),
                pick,
                (((0,), (0,)), ((), ())),
                preferred_element_type=jnp.float32,
            )
            weights.append((both_parts[:ROWS] + both_parts[ROWS:])[None])
        weight = jnp.concatenate(weights, axis=0)
        for n in range(2):
            gate_val = acc[n, g]
            value = gate_val / (1.0 + jnp.exp(-gate_val)) * acc[2 + n, g]
            value = value * weight[:, :, n * UNITS : (n + 1) * UNITS]
            where = pl.ds(pl.multiple_of(c * (2 * UNITS) + n * UNITS, 128), UNITS)
            h[g, :, :, where] = value.astype(jnp.bfloat16)
        send(("h", q), h.at[g, :, :, own_units], h.at[g, :, :, own_units], sibling)

    for q in (3, 1, 2, 0):
        activate(q)
    settle()
    down_load.wait()
    arrived(("wd",), wd.at[other])
    for q in (3, 1, 2, 0):
        arrived(("h", q), h.at[big_at(0, q), :, :, other_units])

    FAR, NEXT, PREV, MINE = 0, 1, 2, 3

    def stage(k, slot):
        return x.at[k, 0, slot]

    def partial(k, q, first, width, slot, add=None):
        g = big_at(k, q)

        def one(n, carry):
            start = pl.multiple_of(first + n * 256, 128)
            cols = pl.ds(start, 256)
            left = h[g] if k == 0 else h[:, g]
            right = wd[:, :, :, pl.ds(pl.multiple_of(k * PART + start, 128), 256)]
            part = jnp.dot(
                left.reshape(SIDE * ROWS, 4 * UNITS),
                right.reshape(4 * UNITS, 256),
                preferred_element_type=jnp.float32,
            ).reshape(SIDE, ROWS, 256)
            if add == "low":
                x[k, 0, slot, :, LOW, cols] = (
                    part[:, :HALF] + half_in[k, 0, :, :, cols].astype(jnp.float32)
                ).astype(jnp.bfloat16)
                x[k, 0, slot, :, HIGH, cols] = part[:, HALF:].astype(jnp.bfloat16)
            elif add == "high":
                x[k, 0, slot, :, LOW, cols] = part[:, :HALF].astype(jnp.bfloat16)
                x[k, 0, slot, :, HIGH, cols] = (
                    part[:, HALF:] + half_in[k, 1, :, :, cols].astype(jnp.float32)
                ).astype(jnp.bfloat16)
            else:
                if add == "both":
                    part = part + full_in[k, 0, :, :, cols].astype(jnp.float32)
                    part = part + full_in[k, 1, :, :, cols].astype(jnp.float32)
                x[k, 0, slot, :, :, cols] = part.astype(jnp.bfloat16)
            return carry

        lax.fori_loop(0, width // 256, one, 0)

    def gather_sum(ref, *others):
        total = ref[...].astype(jnp.float32)
        for one in others:
            total = total + one[...].astype(jnp.float32)
        ref[...] = total.astype(jnp.bfloat16)

    def own_of(d):
        return pl.ds(pl.multiple_of(FIRST + OWN * ((z + d) % SIDE), OWN), OWN)

    def piece(s):
        return own_of(0) if s == 2 else pl.ds(*SUBS[s])

    def z_first(k, i, slots, qs):
        for slot, q in zip(slots, qs):
            partial(k, q, FIRST, SIDE * OWN, slot)
        where = pl.ds(slots[0], len(slots))
        for d in (2, 1, 3):
            send(
                ("zq", k, i, d),
                x.at[k, 0, where, :, :, own_of(d)],
                z_first_in.at[k, d - 1, where],
                at(dz=d),
            )

    def z_first_sum(k, i, slots):
        where = pl.ds(slots[0], len(slots))
        for d in (1, 2, 3):
            arrived(("zq", k, i, d), z_first_in.at[k, d - 1, where])
        for slot in slots:
            gather_sum(
                x.at[k, 0, slot, :, :, own_of(0)],
                *[z_first_in.at[k, d, slot] for d in range(3)],
            )

    def back_far(k, s):
        if s < 2:
            partial(k, 3, *SUBS[s], FAR)
        cols = piece(s)
        send(
            ("rhp", k, s),
            stage(k, FAR).at[:, LOW, cols],
            half_in.at[k, 0, :, :, cols],
            big_next[k],
        )
        send(
            ("rhm", k, s),
            stage(k, FAR).at[:, HIGH, cols],
            half_in.at[k, 1, :, :, cols],
            big_prev[k],
        )

    def back_near(k, s):
        cols = piece(s)
        arrived(("rhp", k, s), half_in.at[k, 0, :, :, cols])
        if s < 2:
            partial(k, 2, *SUBS[s], NEXT, "low")
        else:
            gather_sum(stage(k, NEXT).at[:, LOW, cols], half_in.at[k, 0, :, :, cols])
        send(("rfp", k, s), stage(k, NEXT).at[:, :, cols], full_in.at[k, 0, :, :, cols], big_next[k])
        arrived(("rhm", k, s), half_in.at[k, 1, :, :, cols])
        if s < 2:
            partial(k, 1, *SUBS[s], PREV, "high")
        else:
            gather_sum(stage(k, PREV).at[:, HIGH, cols], half_in.at[k, 1, :, :, cols])
        send(("rfm", k, s), stage(k, PREV).at[:, :, cols], full_in.at[k, 1, :, :, cols], big_prev[k])

    def back_mine(k, s):
        cols = piece(s)
        arrived(("rfp", k, s), full_in.at[k, 0, :, :, cols])
        arrived(("rfm", k, s), full_in.at[k, 1, :, :, cols])
        if s < 2:
            partial(k, 0, *SUBS[s], MINE, "both")
        else:
            gather_sum(
                stage(k, MINE).at[:, :, cols],
                full_in.at[k, 0, :, :, cols],
                full_in.at[k, 1, :, :, cols],
            )
        far = stage(k, MINE).at[small_at(k, 3)]
        send(("thp", k, s), far.at[LOW, cols], small_half_in.at[k, 0, :, cols], small_next[k])
        send(("thm", k, s), far.at[HIGH, cols], small_half_in.at[k, 1, :, cols], small_prev[k])

    def back_small(k, s):
        cols = piece(s)
        arrived(("thp", k, s), small_half_in.at[k, 0, :, cols])
        block = stage(k, MINE).at[small_at(k, 2)]
        gather_sum(block.at[LOW, cols], small_half_in.at[k, 0, :, cols])
        send(("tfp", k, s), block.at[:, cols], small_full_in.at[k, 0, :, cols], small_next[k])
        arrived(("thm", k, s), small_half_in.at[k, 1, :, cols])
        block = stage(k, MINE).at[small_at(k, 1)]
        gather_sum(block.at[HIGH, cols], small_half_in.at[k, 1, :, cols])
        send(("tfm", k, s), block.at[:, cols], small_full_in.at[k, 1, :, cols], small_prev[k])

    def z_rows(d):
        return pl.ds(pl.multiple_of(((z + d) % SIDE) * QUARTER, QUARTER), QUARTER)

    def back_block(k, s):
        cols = piece(s)
        arrived(("tfp", k, s), small_full_in.at[k, 0, :, cols])
        arrived(("tfm", k, s), small_full_in.at[k, 1, :, cols])
        total = (
            x[k, 0, MINE, small[k], :, cols].astype(jnp.float32)
            + small_full_in[k, 0, :, cols].astype(jnp.float32)
            + small_full_in[k, 1, :, cols].astype(jnp.float32)
        ).astype(jnp.bfloat16)
        if s == 2:
            final[k, :, cols] = total
            mine = final.at[k, :, cols]
            for d in (2, 1, 3):
                send(("f", k, s, d), mine, mine, at(dz=d))
            return
        own_sum[k, :, cols] = total
        for d in (2, 1, 3):
            send(
                ("z", k, s, d),
                own_sum.at[k, z_rows(d), cols],
                z_in.at[k, d - 1, :, cols],
                at(dz=d),
            )

    def back_z(k, s):
        cols = piece(s)
        for d in (1, 2, 3):
            arrived(("z", k, s, d), z_in.at[k, d - 1, :, cols])
        total = own_sum[k, z_rows(0), cols].astype(jnp.float32)
        for d in (1, 2, 3):
            total = total + z_in[k, d - 1, :, cols].astype(jnp.float32)
        final[k, z_rows(0), cols] = total.astype(jnp.bfloat16)
        for d in (2, 1, 3):
            mine = final.at[k, z_rows(0), cols]
            send(("f", k, s, d), mine, mine, at(dz=d))

    last = []

    def columns_of(s):
        return (FIRST, SIDE * OWN) if s == 2 else SUBS[s]

    def back_out(k, s):
        for d in (1, 2, 3):
            if s == 2:
                landing = final.at[k, :, own_of(SIDE - d)]
            else:
                landing = final.at[k, z_rows(SIDE - d), piece(s)]
            arrived(("f", k, s, d), landing)
        first, width = columns_of(s)
        where = pl.ds(pl.multiple_of(c * (2 * PART) + k * PART + first, 128), width)
        src = final.at[k, :, pl.ds(first, width)]
        send(("o", k, s), src, out.at[:, where], sibling)
        last.append(local(src, out.at[:, where]))

    def back_sibling(k, s):
        first, width = columns_of(s)
        where = pl.ds(pl.multiple_of(other * (2 * PART) + k * PART + first, 128), width)
        arrived(("o", k, s), out.at[:, where])

    def lat_from_z():
        for d in (1, 2, 3):
            arrived(("lz", d), lat.at[c, :, :, (z + SIDE - d) % SIDE])
        lat[c, :, :, z] = side[c, :, :, :, LAT_COLS]
        send(("lc",), lat.at[c], lat.at[c], sibling)

    def place_latents():
        arrived(("lc",), lat.at[other])
        me = (e * (2 * SIDE) + hid).astype(jnp.float32)
        seek = lax.broadcasted_iota(jnp.int32, (8, LAT_PART), 1) == LAT_PART - 1
        seek = seek.astype(jnp.bfloat16)
        before = lax.broadcasted_iota(jnp.int32, (128, 128), 0)
        before = before < lax.broadcasted_iota(jnp.int32, (128, 128), 1)
        before = before.astype(jnp.bfloat16)
        slot = lax.broadcasted_iota(jnp.int32, (SLOTS, 128), 0).astype(jnp.float32)
        taken = jnp.zeros((8, 1), jnp.float32)
        sums = [jnp.zeros((SLOTS, LAT_PART), jnp.float32) for _ in range(2)]
        for yy in range(SIDE):
            for pair_of in range(2):
                rows = [
                    lat[core, yy, 2 * pair_of : 2 * pair_of + 2].reshape(128, LAT_PART)
                    for core in range(2)
                ]
                owner = lax.dot_general(
                    seek, rows[1], (((1,), (1,)), ((), ())), preferred_element_type=jnp.float32
                )
                mine = (owner == me).astype(jnp.float32)
                earlier = taken + jnp.dot(
                    mine.astype(jnp.bfloat16), before, preferred_element_type=jnp.float32
                )
                taken = taken + jnp.sum(mine, axis=1, keepdims=True)
                place = jnp.where(earlier[:1] == slot, mine[:1], 0.0).astype(jnp.bfloat16)
                for core in range(2):
                    sums[core] = sums[core] + jnp.dot(
                        place, rows[core], preferred_element_type=jnp.float32
                    )
        cache[:, :LAT_PART] = sums[0].astype(jnp.bfloat16)
        cache[:, LAT_PART:] = sums[1][:, : LAT - LAT_PART].astype(jnp.bfloat16)

    both = (0, 1)

    def do(step, s):
        for k in both:
            step(k, s)

    do(back_far, 0)
    for k in both:
        z_first(k, 0, (FAR,), (3,))
    do(back_far, 1)
    for k in both:
        z_first(k, 1, (NEXT, PREV), (2, 1))
    do(back_near, 0)
    for k in both:
        z_first(k, 2, (MINE,), (0,))
    lat_from_z()
    do(back_near, 1)
    for k in both:
        z_first_sum(k, 0, (FAR,))
    do(back_far, 2)
    place_latents()
    do(back_mine, 0)
    for k in both:
        z_first_sum(k, 1, (NEXT, PREV))
    do(back_near, 2)
    do(back_mine, 1)
    do(back_small, 0)
    for k in both:
        z_first_sum(k, 2, (MINE,))
    do(back_mine, 2)
    do(back_small, 1)
    do(back_block, 0)
    do(back_small, 2)
    do(back_block, 1)
    do(back_z, 0)
    do(back_block, 2)
    do(back_z, 1)
    do(back_out, 0)
    do(back_out, 2)
    do(back_out, 1)
    for s in (0, 2, 1):
        do(back_sibling, s)
    for copy in last:
        copy.wait()
    settle()


def layer(tokens, routes, route_weights, gate, up, down, latents, kv_gain, owners):
    bf16 = jnp.bfloat16
    anywhere = pl.BlockSpec(memory_space=pl.ANY)
    vmem = pl.BlockSpec(memory_space=pltpu.VMEM)
    smem = pl.BlockSpec(memory_space=pltpu.SMEM)
    return pl.pallas_call(
        moe_kernel,
        out_shape=(
            jax.ShapeDtypeStruct((ROWS, WIDE), bf16),
            jax.ShapeDtypeStruct((SLOTS, LAT), bf16),
        ),
        in_specs=[anywhere, vmem, vmem, anywhere, anywhere, anywhere, vmem, vmem, smem],
        out_specs=(anywhere, vmem),
        scratch_shapes=[
            pltpu.VMEM((2, 2, SIDE, SIDE, ROWS, PART), bf16),
            pltpu.VMEM((4, WIDE, UNITS), bf16),
            pltpu.VMEM((2, 2, UNITS, 2 * PART), bf16),
            pltpu.VMEM((4, SIDE, SIDE, ROWS, UNITS), jnp.float32),
            pltpu.VMEM((SIDE, SIDE, ROWS, 4 * UNITS), bf16),
            pltpu.VMEM((2, 8, 2 * LAT_PART), jnp.float32),
            pltpu.VMEM((2, SIDE, SIDE, QUARTER, SIDE_COLS), bf16),
            pltpu.VMEM((2, SIDE, SIDE, SIDE, QUARTER, LAT_PART), bf16),
            pltpu.VMEM((2, 3, SIDE, SIDE, ROWS, OWN), bf16),
            pltpu.VMEM((2, 2, SIDE, HALF, PART), bf16),
            pltpu.VMEM((2, 2, SIDE, ROWS, PART), bf16),
            pltpu.VMEM((2, 2, HALF, PART), bf16),
            pltpu.VMEM((2, 2, ROWS, PART), bf16),
            pltpu.VMEM((2, ROWS, PART), bf16),
            pltpu.VMEM((2, 3, QUARTER, PART), bf16),
            pltpu.VMEM((2, ROWS, PART), bf16),
            pltpu.SemaphoreType.DMA((N_SEMS,)),
            pltpu.SemaphoreType.DMA((N_SEMS,)),
            pltpu.SemaphoreType.DMA((16,)),
        ],
        compiler_params=pltpu.CompilerParams(
            collective_id=0, has_side_effects=True, vmem_limit_bytes=60 << 20
        ),
        cost_estimate=pl.CostEstimate(
            flops=2 * 3 * 1024 * WIDE * 512, bytes_accessed=24 << 20, transcendentals=1 << 19
        ),
        name="moe",
    )(tokens, routes, route_weights, gate, up, down, latents, kv_gain, owners)


def body(tokens, routes, route_weights, gate_proj, up_proj, down_proj, latents, kv_gain, owners):
    return layer(
        tokens,
        routes.T,
        route_weights.T,
        gate_proj,
        up_proj,
        down_proj,
        latents,
        kv_gain.reshape(1, KV_RANK),
        owners,
    )


def solution(mesh):
    return jax.shard_map(
        body,
        mesh=mesh,
        in_specs=(
            P("expert", None),
            P("expert", None),
            P("expert", None),
            P("expert", None, "hidden"),
            P("expert", None, "hidden"),
            P("expert", "hidden", None),
            P(("expert", "hidden"), None),
            P(),
            P(("expert", "hidden")),
        ),
        out_specs=(P("expert", None), P(("expert", "hidden"), None)),
        check_vma=False,
    )
```

```python
import functools

import jax
import jax.numpy as jnp
from jax import lax
from jax.experimental import pallas as pl
from jax.experimental.pallas import tpu as pltpu
from jax.sharding import PartitionSpec as P

KV_RANK = 512
LAT = 576
LAT_PART = 384
LAT_COLS = pl.ds(0, LAT_PART)
SIDE_COLS = 512
SLOTS = 16
N_EXPERTS = 32
TOP = 8
SIDE = 4
ROWS = 64
HALF = 32
QUARTER = 16
WIDE = 7168
PART = 1792
UNITS = 256
N_SEMS = 256
SUBS = ((0, 768), (768, 512))
FIRST = 1280
OWN = 128

MESH = pl.DeviceIdType.MESH


def moe_kernel(
    tokens,
    routes,
    route_weights,
    gate,
    up,
    down,
    latents,
    kv_gain,
    owners,
    out,
    cache,
    x,
    w,
    wd,
    acc,
    h,
    normed,
    side,
    lat,
    z_first_in,
    half_in,
    full_in,
    small_half_in,
    small_full_in,
    own_sum,
    z_in,
    final,
    send_sems,
    recv_sems,
    local_sems,
):
    e = lax.axis_index("expert")
    hid = lax.axis_index("hidden")
    y, xx, z, c = e // SIDE, e % SIDE, hid // 2, hid % 2
    other = 1 - c

    def at(dy=0, dx=0, dz=0, flip=False):
        core = other if flip else c
        return (
            ((y + dy) % SIDE) * SIDE + (xx + dx) % SIDE,
            ((z + dz) % SIDE) * 2 + core,
        )

    x_next, x_prev = at(dx=1), at(dx=3)
    y_next, y_prev = at(dy=1), at(dy=3)
    sibling = at(flip=True)

    keys = {}

    def sem_of(key):
        if key not in keys:
            keys[key] = len(keys)
            assert len(keys) <= N_SEMS
        return keys[key]

    pending = []

    def send(key, src, dst, device):
        i = sem_of(key)
        copy = pltpu.make_async_remote_copy(
            src_ref=src,
            dst_ref=dst,
            send_sem=send_sems.at[i],
            recv_sem=recv_sems.at[i],
            device_id=device,
            device_id_type=MESH,
        )
        copy.start()
        pending.append(copy)

    def arrived(key, landing):
        i = sem_of(key)
        pltpu.make_async_remote_copy(
            src_ref=landing,
            dst_ref=landing,
            send_sem=send_sems.at[i],
            recv_sem=recv_sems.at[i],
            device_id=sibling,
            device_id_type=MESH,
        ).wait_recv()

    def settle():
        for copy in pending:
            copy.wait_send()
        pending.clear()

    locals_ = []

    def local(src, dst):
        copy = pltpu.make_async_copy(src, dst, local_sems.at[len(locals_)])
        copy.start()
        locals_.append(copy)
        return copy

    big = (y, xx)
    small = (xx, y)
    big_next, big_prev = (y_next, x_next), (y_prev, x_prev)
    small_next, small_prev = (x_next, y_next), (x_prev, y_prev)
    STEP = (0, 3, 1, 2)

    def big_at(k, q):
        return (big[k] + STEP[q]) % SIDE

    def small_at(k, r):
        return (small[k] + STEP[r]) % SIDE

    def token_columns(k, half):
        return pl.ds(pl.multiple_of(half * (2 * PART) + k * PART, 128), PART)

    LOW, HIGH = pl.ds(0, HALF), pl.ds(HALF, HALF)

    weight_loads = [local(gate, w.at[pl.ds(0, 2)]), local(up, w.at[pl.ds(2, 2)])]
    token_loads = [
        local(tokens.at[:, token_columns(k, half)], x.at[k, half, big[k], small[k]])
        for k in range(2)
        for half in range(2)
    ]

    chosen = routes[...]
    strength = route_weights[...]
    expert_row = lax.broadcasted_iota(jnp.int32, (N_EXPERTS, ROWS), 0)
    dense = jnp.zeros((N_EXPERTS, ROWS), jnp.float32)
    for j in range(TOP):
        dense = dense + jnp.where(expert_row == chosen[j : j + 1], strength[j : j + 1], 0.0)
    dense_high = dense.astype(jnp.bfloat16).astype(jnp.float32)
    packed = jnp.concatenate([dense_high, dense - dense_high], axis=1)
    packed = jnp.where(c == 0, packed[:QUARTER], packed[QUARTER:])

    head = latents[:, :KV_RANK].astype(jnp.float32)
    tail = latents[:, KV_RANK:].astype(jnp.float32)
    scale = lax.rsqrt(jnp.sum(head * head, axis=1, keepdims=True) / KV_RANK + 1e-06)
    lat_rows = latents.shape[0]
    row = lax.broadcasted_iota(jnp.int32, (lat_rows, 2 * LAT_PART - LAT), 0)
    marks = jnp.zeros(row.shape, jnp.float32)
    for i in range(lat_rows):
        marks = jnp.where(row == i, owners[i].astype(jnp.float32), marks)
    normed[0, :, :KV_RANK] = head * scale * kv_gain[...]
    normed[0, :, KV_RANK:] = jnp.concatenate([tail, marks], axis=1)
    acc[...] = jnp.zeros_like(acc)

    barrier = pltpu.get_barrier_semaphore()
    partners = (x_next, x_prev, y_next, y_prev, at(dz=1), at(dz=2), at(dz=3), sibling)
    for partner in partners:
        pl.semaphore_signal(barrier, inc=1, device_id=partner, device_id_type=MESH)
    pl.semaphore_wait(barrier, len(partners))

    def block(k, q, r):
        return x.at[k, c, big_at(k, q), small_at(k, r)]

    def send_block(key, k, q, r, device, rows=None):
        ref = block(k, q, r)
        if rows is not None:
            ref = ref.at[rows]
        send(key, ref, ref, device)

    def block_arrived(key, k, q, r, rows=None):
        ref = block(k, q, r)
        if rows is not None:
            ref = ref.at[rows]
        arrived(key, ref)

    def send_own(key, k, device):
        send(key, tokens.at[:, token_columns(k, c)], block(k, 0, 0), device)

    SIDE_LEFT, SIDE_RIGHT = pl.ds(0, SIDE_COLS // 2), pl.ds(SIDE_COLS // 2, SIDE_COLS // 2)

    def side_ref(dy=0, dx=0):
        return side.at[c, (y + dy) % SIDE, (xx + dx) % SIDE]

    def side_row(dy=0):
        return side.at[c, (y + dy) % SIDE]

    def side_one():
        arrived(("n",), normed.at[1])
        first = jnp.where(c == 0, normed[0], normed[1])
        second = jnp.where(c == 0, normed[1], normed[0])
        pair = jnp.concatenate([first, second], axis=0)
        pair = jnp.where(c == 0, pair[:, :LAT_PART], pair[:, LAT_PART:])
        side[c, y, xx] = jnp.concatenate([pair, packed], axis=1).astype(jnp.bfloat16)
        send(("g1p",), side_ref(), side_ref(), x_next)
        send(("g1m",), side_ref(), side_ref(), x_prev)

    def side_two():
        arrived(("g1p",), side_ref(dx=3))
        ref = side_ref(dx=3).at[:, SIDE_LEFT]
        send(("g2p",), ref, ref, x_next)
        arrived(("g1m",), side_ref(dx=1))
        ref = side_ref(dx=1).at[:, SIDE_RIGHT]
        send(("g2m",), ref, ref, x_prev)

    def side_three():
        arrived(("g2p",), side_ref(dx=2).at[:, SIDE_LEFT])
        arrived(("g2m",), side_ref(dx=2).at[:, SIDE_RIGHT])
        send(("g3p",), side_row(), side_row(), y_next)
        send(("g3m",), side_row(), side_row(), y_prev)

    def side_four():
        arrived(("g3p",), side_row(3))
        ref = side_row(3).at[:, :, SIDE_LEFT]
        send(("g4p",), ref, ref, y_next)
        arrived(("g3m",), side_row(1))
        ref = side_row(1).at[:, :, SIDE_RIGHT]
        send(("g4m",), ref, ref, y_prev)

    def side_done():
        arrived(("g4p",), side_row(2).at[:, :, SIDE_LEFT])
        arrived(("g4m",), side_row(2).at[:, :, SIDE_RIGHT])
        send(("gc",), side.at[c], side.at[c], sibling)
        for d in (2, 1, 3):
            send(("lz", d), side.at[c, :, :, :, LAT_COLS], lat.at[c, :, :, z], at(dz=d))

    def to_sibling(k, q, r):
        send(("c", k, q, r), block(k, q, r), block(k, q, r), sibling)

    def from_sibling(k, q, r):
        arrived(("c", k, q, r), x.at[k, other, big_at(k, q), small_at(k, r)])

    send(("n",), normed.at[0], normed.at[1], sibling)
    for k in (1, 0):
        send_own(("s1p", k), k, small_next[k])
        send_own(("s1m", k), k, small_prev[k])
    for k in (0, 1):
        send_own(("b1p", k, 0), k, big_next[k])
        send_own(("b1m", k, 0), k, big_prev[k])
    side_one()
    down_half = pl.ds(pl.multiple_of(c * (2 * PART), 128), 2 * PART)
    down_other = pl.ds(pl.multiple_of(other * (2 * PART), 128), 2 * PART)
    send(("wd",), down.at[:, :, down_other], wd.at[c], sibling)
    down_load = local(down.at[:, :, down_half], wd.at[c])

    for k in (0, 1):
        block_arrived(("s1p", k), k, 0, 1)
        send_block(("s2p", k), k, 0, 1, small_next[k], LOW)
        block_arrived(("s1m", k), k, 0, 2)
        send_block(("s2m", k), k, 0, 2, small_prev[k], HIGH)
    for r in (1, 2):
        for k in (0, 1):
            send_block(("b1p", k, r), k, 0, r, big_next[k])
            send_block(("b1m", k, r), k, 0, r, big_prev[k])
            to_sibling(k, 0, r)
    for k in (0, 1):
        block_arrived(("s2p", k), k, 0, 3, LOW)
        block_arrived(("s2m", k), k, 0, 3, HIGH)
        send_block(("b1p", k, 3), k, 0, 3, big_next[k])
        send_block(("b1m", k, 3), k, 0, 3, big_prev[k])
        to_sibling(k, 0, 3)
    side_two()

    def long_step(r):
        for k in (0, 1):
            block_arrived(("b1p", k, r), k, 1, r)
            send_block(("b2p", k, r), k, 1, r, big_next[k], LOW)
            block_arrived(("b1m", k, r), k, 2, r)
            send_block(("b2m", k, r), k, 2, r, big_prev[k], HIGH)
            to_sibling(k, 1, r)
            to_sibling(k, 2, r)

    def far_step(r):
        for k in (0, 1):
            block_arrived(("b2p", k, r), k, 3, r, LOW)
            block_arrived(("b2m", k, r), k, 3, r, HIGH)
            to_sibling(k, 3, r)

    def multiply(k, half, blocks):
        start = half * (2 * PART) + k * PART
        places = [(big_at(k, q), small_at(k, r)) for q, r in blocks]

        left = jnp.concatenate([x[k, half, g, j] for g, j in places], axis=0)
        for n in range(4):
            right = w[n, pl.ds(pl.multiple_of(start, 128), PART), :]
            part = jnp.dot(left, right, preferred_element_type=jnp.float32)
            for i, (g, j) in enumerate(places):
                piece = part[i * ROWS : (i + 1) * ROWS]
                if k == 0:
                    acc[n, g, j] += piece
                else:
                    acc[n, j, g] += piece

    NEAR_ROW = ((0, 0), (0, 1), (0, 2), (0, 3))
    EARLY = ((1, 0), (1, 1), (2, 0), (2, 1))
    LATE = ((1, 2), (1, 3), (2, 2), (2, 3))
    FAR_ROW = ((3, 0), (3, 1), (3, 2), (3, 3))

    def rest(k, blocks):
        for q, r in blocks:
            if (q, r) != (0, 0):
                from_sibling(k, q, r)
        multiply(k, other, blocks)

    for copy in weight_loads + token_loads:
        copy.wait()
    long_step(0)
    for k in (0, 1):
        multiply(k, c, NEAR_ROW)
    side_three()
    long_step(1)
    for k in (0, 1):
        rest(k, NEAR_ROW)
    for k in (0, 1):
        multiply(k, c, EARLY)
    long_step(2)
    for k in (0, 1):
        rest(k, EARLY)
    side_four()
    long_step(3)
    far_step(0)
    for k in (0, 1):
        multiply(k, c, LATE)
    far_step(1)
    for k in (0, 1):
        rest(k, LATE)
    side_done()
    far_step(2)
    far_step(3)
    for k in (0, 1):
        multiply(k, c, FAR_ROW)
    for k in (0, 1):
        rest(k, FAR_ROW)

    expert = lax.broadcasted_iota(jnp.int32, (N_EXPERTS, 2 * UNITS), 0)
    column = lax.broadcasted_iota(jnp.int32, (N_EXPERTS, 2 * UNITS), 1)
    pick = (expert == 2 * e + column // UNITS).astype(jnp.bfloat16)
    arrived(("gc",), side.at[other])
    own_units = pl.ds(pl.multiple_of(c * (2 * UNITS), 128), 2 * UNITS)
    other_units = pl.ds(pl.multiple_of(other * (2 * UNITS), 128), 2 * UNITS)

    def activate(q):
        g = big_at(0, q)
        weights = []
        for j in range(SIDE):
            halves = [side[core, g, j, :, 3 * 128 :] for core in range(2)]
            both_parts = lax.dot_general(
                jnp.concatenate(halves, axis=0),
                pick,
                (((0,), (0,)), ((), ())),
                preferred_element_type=jnp.float32,
            )
            weights.append((both_parts[:ROWS] + both_parts[ROWS:])[None])
        weight = jnp.concatenate(weights, axis=0)
        for n in range(2):
            gate_val = acc[n, g]
            value = gate_val / (1.0 + jnp.exp(-gate_val)) * acc[2 + n, g]
            value = value * weight[:, :, n * UNITS : (n + 1) * UNITS]
            where = pl.ds(pl.multiple_of(c * (2 * UNITS) + n * UNITS, 128), UNITS)
            h[g, :, :, where] = value.astype(jnp.bfloat16)
        send(("h", q), h.at[g, :, :, own_units], h.at[g, :, :, own_units], sibling)

    for q in (3, 1, 2, 0):
        activate(q)
    settle()
    down_load.wait()
    arrived(("wd",), wd.at[other])
    for q in (3, 1, 2, 0):
        arrived(("h", q), h.at[big_at(0, q), :, :, other_units])

    FAR, NEXT, PREV, MINE = 0, 1, 2, 3

    def stage(k, slot):
        return x.at[k, 0, slot]

    def partial(k, q, first, width, slot, add=None):
        g = big_at(k, q)

        left = h[g] if k == 0 else h[:, g]
        left = left.reshape(SIDE * ROWS, 4 * UNITS)
        for start in range(first, first + width, 256):
            cols = pl.ds(start, 256)
            right = wd[:, :, :, pl.ds(k * PART + start, 256)].reshape(4 * UNITS, 256)
            part = jnp.dot(left, right, preferred_element_type=jnp.float32)
            part = part.reshape(SIDE, ROWS, 256)
            if add == "low":
                x[k, 0, slot, :, LOW, cols] = (
                    part[:, :HALF] + half_in[k, 0, :, :, cols].astype(jnp.float32)
                ).astype(jnp.bfloat16)
                x[k, 0, slot, :, HIGH, cols] = part[:, HALF:].astype(jnp.bfloat16)
            elif add == "high":
                x[k, 0, slot, :, LOW, cols] = part[:, :HALF].astype(jnp.bfloat16)
                x[k, 0, slot, :, HIGH, cols] = (
                    part[:, HALF:] + half_in[k, 1, :, :, cols].astype(jnp.float32)
                ).astype(jnp.bfloat16)
            else:
                if add == "both":
                    part = part + full_in[k, 0, :, :, cols].astype(jnp.float32)
                    part = part + full_in[k, 1, :, :, cols].astype(jnp.float32)
                x[k, 0, slot, :, :, cols] = part.astype(jnp.bfloat16)

    def gather_sum(ref, *others):
        total = ref[...].astype(jnp.float32)
        for one in others:
            total = total + one[...].astype(jnp.float32)
        ref[...] = total.astype(jnp.bfloat16)

    def own_of(d):
        return pl.ds(pl.multiple_of(FIRST + OWN * ((z + d) % SIDE), OWN), OWN)

    def piece(s):
        return own_of(0) if s == 2 else pl.ds(*SUBS[s])

    def z_first(k, i, slots, qs):
        for slot, q in zip(slots, qs):
            partial(k, q, FIRST, SIDE * OWN, slot)
        where = pl.ds(slots[0], len(slots))
        for d in (2, 1, 3):
            send(
                ("zq", k, i, d),
                x.at[k, 0, where, :, :, own_of(d)],
                z_first_in.at[k, d - 1, where],
                at(dz=d),
            )

    def z_first_sum(k, i, slots):
        where = pl.ds(slots[0], len(slots))
        for d in (1, 2, 3):
            arrived(("zq", k, i, d), z_first_in.at[k, d - 1, where])
        for slot in slots:
            gather_sum(
                x.at[k, 0, slot, :, :, own_of(0)],
                *[z_first_in.at[k, d, slot] for d in range(3)],
            )

    def back_far(k, s):
        if s < 2:
            partial(k, 3, *SUBS[s], FAR)
        cols = piece(s)
        send(
            ("rhp", k, s),
            stage(k, FAR).at[:, LOW, cols],
            half_in.at[k, 0, :, :, cols],
            big_next[k],
        )
        send(
            ("rhm", k, s),
            stage(k, FAR).at[:, HIGH, cols],
            half_in.at[k, 1, :, :, cols],
            big_prev[k],
        )

    def back_near(k, s):
        cols = piece(s)
        arrived(("rhp", k, s), half_in.at[k, 0, :, :, cols])
        if s < 2:
            partial(k, 2, *SUBS[s], NEXT, "low")
        else:
            gather_sum(stage(k, NEXT).at[:, LOW, cols], half_in.at[k, 0, :, :, cols])
        send(("rfp", k, s), stage(k, NEXT).at[:, :, cols], full_in.at[k, 0, :, :, cols], big_next[k])
        arrived(("rhm", k, s), half_in.at[k, 1, :, :, cols])
        if s < 2:
            partial(k, 1, *SUBS[s], PREV, "high")
        else:
            gather_sum(stage(k, PREV).at[:, HIGH, cols], half_in.at[k, 1, :, :, cols])
        send(("rfm", k, s), stage(k, PREV).at[:, :, cols], full_in.at[k, 1, :, :, cols], big_prev[k])

    def back_mine(k, s):
        cols = piece(s)
        arrived(("rfp", k, s), full_in.at[k, 0, :, :, cols])
        arrived(("rfm", k, s), full_in.at[k, 1, :, :, cols])
        if s < 2:
            partial(k, 0, *SUBS[s], MINE, "both")
        else:
            gather_sum(
                stage(k, MINE).at[:, :, cols],
                full_in.at[k, 0, :, :, cols],
                full_in.at[k, 1, :, :, cols],
            )
        far = stage(k, MINE).at[small_at(k, 3)]
        send(("thp", k, s), far.at[LOW, cols], small_half_in.at[k, 0, :, cols], small_next[k])
        send(("thm", k, s), far.at[HIGH, cols], small_half_in.at[k, 1, :, cols], small_prev[k])

    def back_small(k, s):
        cols = piece(s)
        arrived(("thp", k, s), small_half_in.at[k, 0, :, cols])
        block = stage(k, MINE).at[small_at(k, 2)]
        gather_sum(block.at[LOW, cols], small_half_in.at[k, 0, :, cols])
        send(("tfp", k, s), block.at[:, cols], small_full_in.at[k, 0, :, cols], small_next[k])
        arrived(("thm", k, s), small_half_in.at[k, 1, :, cols])
        block = stage(k, MINE).at[small_at(k, 1)]
        gather_sum(block.at[HIGH, cols], small_half_in.at[k, 1, :, cols])
        send(("tfm", k, s), block.at[:, cols], small_full_in.at[k, 1, :, cols], small_prev[k])

    def z_rows(d):
        return pl.ds(pl.multiple_of(((z + d) % SIDE) * QUARTER, QUARTER), QUARTER)

    def back_block(k, s):
        cols = piece(s)
        arrived(("tfp", k, s), small_full_in.at[k, 0, :, cols])
        arrived(("tfm", k, s), small_full_in.at[k, 1, :, cols])
        total = (
            x[k, 0, MINE, small[k], :, cols].astype(jnp.float32)
            + small_full_in[k, 0, :, cols].astype(jnp.float32)
            + small_full_in[k, 1, :, cols].astype(jnp.float32)
        ).astype(jnp.bfloat16)
        if s == 2:
            final[k, :, cols] = total
            mine = final.at[k, :, cols]
            for d in (2, 1, 3):
                send(("f", k, s, d), mine, mine, at(dz=d))
            return
        own_sum[k, :, cols] = total
        for d in (2, 1, 3):
            send(
                ("z", k, s, d),
                own_sum.at[k, z_rows(d), cols],
                z_in.at[k, d - 1, :, cols],
                at(dz=d),
            )

    def back_z(k, s):
        cols = piece(s)
        for d in (1, 2, 3):
            arrived(("z", k, s, d), z_in.at[k, d - 1, :, cols])
        total = own_sum[k, z_rows(0), cols].astype(jnp.float32)
        for d in (1, 2, 3):
            total = total + z_in[k, d - 1, :, cols].astype(jnp.float32)
        final[k, z_rows(0), cols] = total.astype(jnp.bfloat16)
        for d in (2, 1, 3):
            mine = final.at[k, z_rows(0), cols]
            send(("f", k, s, d), mine, mine, at(dz=d))

    last = []

    def columns_of(s):
        return (FIRST, SIDE * OWN) if s == 2 else SUBS[s]

    def back_out(k, s):
        for d in (1, 2, 3):
            if s == 2:
                landing = final.at[k, :, own_of(SIDE - d)]
            else:
                landing = final.at[k, z_rows(SIDE - d), piece(s)]
            arrived(("f", k, s, d), landing)
        first, width = columns_of(s)
        where = pl.ds(pl.multiple_of(c * (2 * PART) + k * PART + first, 128), width)
        src = final.at[k, :, pl.ds(first, width)]
        send(("o", k, s), src, out.at[:, where], sibling)
        last.append(local(src, out.at[:, where]))

    def back_sibling(k, s):
        first, width = columns_of(s)
        where = pl.ds(pl.multiple_of(other * (2 * PART) + k * PART + first, 128), width)
        arrived(("o", k, s), out.at[:, where])

    def lat_from_z():
        for d in (1, 2, 3):
            arrived(("lz", d), lat.at[c, :, :, (z + SIDE - d) % SIDE])
        lat[c, :, :, z] = side[c, :, :, :, LAT_COLS]
        send(("lc",), lat.at[c], lat.at[c], sibling)

    def place_latents():
        arrived(("lc",), lat.at[other])
        me = (e * (2 * SIDE) + hid).astype(jnp.float32)
        seek = lax.broadcasted_iota(jnp.int32, (8, LAT_PART), 1) == LAT_PART - 1
        seek = seek.astype(jnp.bfloat16)
        before = lax.broadcasted_iota(jnp.int32, (128, 128), 0)
        before = before < lax.broadcasted_iota(jnp.int32, (128, 128), 1)
        before = before.astype(jnp.bfloat16)
        slot = lax.broadcasted_iota(jnp.int32, (SLOTS, 128), 0).astype(jnp.float32)
        taken = jnp.zeros((8, 1), jnp.float32)
        sums = [jnp.zeros((SLOTS, LAT_PART), jnp.float32) for _ in range(2)]
        for yy in range(SIDE):
            for pair_of in range(2):
                rows = [
                    lat[core, yy, 2 * pair_of : 2 * pair_of + 2].reshape(128, LAT_PART)
                    for core in range(2)
                ]
                owner = lax.dot_general(
                    seek, rows[1], (((1,), (1,)), ((), ())), preferred_element_type=jnp.float32
                )
                mine = (owner == me).astype(jnp.float32)
                earlier = taken + jnp.dot(
                    mine.astype(jnp.bfloat16), before, preferred_element_type=jnp.float32
                )
                taken = taken + jnp.sum(mine, axis=1, keepdims=True)
                place = jnp.where(earlier[:1] == slot, mine[:1], 0.0).astype(jnp.bfloat16)
                for core in range(2):
                    sums[core] = sums[core] + jnp.dot(
                        place, rows[core], preferred_element_type=jnp.float32
                    )
        cache[:, :LAT_PART] = sums[0].astype(jnp.bfloat16)
        cache[:, LAT_PART:] = sums[1][:, : LAT - LAT_PART].astype(jnp.bfloat16)

    both = (0, 1)

    def do(step, s):
        for k in both:
            step(k, s)

    do(back_far, 0)
    for k in both:
        z_first(k, 0, (FAR,), (3,))
    do(back_far, 1)
    for k in both:
        z_first(k, 1, (NEXT, PREV), (2, 1))
    do(back_near, 0)
    for k in both:
        z_first(k, 2, (MINE,), (0,))
    lat_from_z()
    do(back_near, 1)
    for k in both:
        z_first_sum(k, 0, (FAR,))
    do(back_far, 2)
    place_latents()
    do(back_mine, 0)
    for k in both:
        z_first_sum(k, 1, (NEXT, PREV))
    do(back_near, 2)
    do(back_mine, 1)
    do(back_small, 0)
    for k in both:
        z_first_sum(k, 2, (MINE,))
    do(back_mine, 2)
    do(back_small, 1)
    do(back_block, 0)
    do(back_small, 2)
    do(back_block, 1)
    do(back_z, 0)
    do(back_block, 2)
    do(back_z, 1)
    do(back_out, 0)
    do(back_out, 2)
    do(back_out, 1)
    for s in (0, 2, 1):
        do(back_sibling, s)
    for copy in last:
        copy.wait()
    settle()


def layer(tokens, routes, route_weights, gate, up, down, latents, kv_gain, owners):
    bf16 = jnp.bfloat16
    anywhere = pl.BlockSpec(memory_space=pl.ANY)
    vmem = pl.BlockSpec(memory_space=pltpu.VMEM)
    smem = pl.BlockSpec(memory_space=pltpu.SMEM)
    return pl.pallas_call(
        moe_kernel,
        out_shape=(
            jax.ShapeDtypeStruct((ROWS, WIDE), bf16),
            jax.ShapeDtypeStruct((SLOTS, LAT), bf16),
        ),
        in_specs=[anywhere, vmem, vmem, anywhere, anywhere, anywhere, vmem, vmem, smem],
        out_specs=(anywhere, vmem),
        scratch_shapes=[
            pltpu.VMEM((2, 2, SIDE, SIDE, ROWS, PART), bf16),
            pltpu.VMEM((4, WIDE, UNITS), bf16),
            pltpu.VMEM((2, 2, UNITS, 2 * PART), bf16),
            pltpu.VMEM((4, SIDE, SIDE, ROWS, UNITS), jnp.float32),
            pltpu.VMEM((SIDE, SIDE, ROWS, 4 * UNITS), bf16),
            pltpu.VMEM((2, 8, 2 * LAT_PART), jnp.float32),
            pltpu.VMEM((2, SIDE, SIDE, QUARTER, SIDE_COLS), bf16),
            pltpu.VMEM((2, SIDE, SIDE, SIDE, QUARTER, LAT_PART), bf16),
            pltpu.VMEM((2, 3, SIDE, SIDE, ROWS, OWN), bf16),
            pltpu.VMEM((2, 2, SIDE, HALF, PART), bf16),
            pltpu.VMEM((2, 2, SIDE, ROWS, PART), bf16),
            pltpu.VMEM((2, 2, HALF, PART), bf16),
            pltpu.VMEM((2, 2, ROWS, PART), bf16),
            pltpu.VMEM((2, ROWS, PART), bf16),
            pltpu.VMEM((2, 3, QUARTER, PART), bf16),
            pltpu.VMEM((2, ROWS, PART), bf16),
            pltpu.SemaphoreType.DMA((N_SEMS,)),
            pltpu.SemaphoreType.DMA((N_SEMS,)),
            pltpu.SemaphoreType.DMA((16,)),
        ],
        compiler_params=pltpu.CompilerParams(
            collective_id=0, has_side_effects=True, vmem_limit_bytes=60 << 20
        ),
        cost_estimate=pl.CostEstimate(
            flops=2 * 3 * 1024 * WIDE * 512, bytes_accessed=24 << 20, transcendentals=1 << 19
        ),
        name="moe",
    )(tokens, routes, route_weights, gate, up, down, latents, kv_gain, owners)


def body(tokens, routes, route_weights, gate_proj, up_proj, down_proj, latents, kv_gain, owners):
    return layer(
        tokens,
        routes.T,
        route_weights.T,
        gate_proj,
        up_proj,
        down_proj,
        latents,
        kv_gain.reshape(1, KV_RANK),
        owners,
    )


def solution(mesh):
    return jax.shard_map(
        body,
        mesh=mesh,
        in_specs=(
            P("expert", None),
            P("expert", None),
            P("expert", None),
            P("expert", None, "hidden"),
            P("expert", None, "hidden"),
            P("expert", "hidden", None),
            P(("expert", "hidden"), None),
            P(),
            P(("expert", "hidden")),
        ),
        out_specs=(P("expert", None), P(("expert", "hidden"), None)),
        check_vma=False,
    )
```

```python
import functools

import jax
import jax.numpy as jnp
from jax import lax
from jax.experimental import pallas as pl
from jax.experimental.pallas import tpu as pltpu
from jax.sharding import PartitionSpec as P

KV_RANK = 512
LAT = 576
LAT_PART = 384
LAT_COLS = pl.ds(0, LAT_PART)
SIDE_COLS = 512
SLOTS = 16
N_EXPERTS = 32
TOP = 8
SIDE = 4
ROWS = 64
HALF = 32
QUARTER = 16
WIDE = 7168
PART = 1792
UNITS = 256
N_SEMS = 256
SUBS = ((0, 512), (512, 768))
FIRST = 1280
OWN = 128

MESH = pl.DeviceIdType.MESH


def moe_kernel(
    tokens,
    routes,
    route_weights,
    gate,
    up,
    down,
    latents,
    kv_gain,
    owners,
    out,
    cache,
    x,
    w,
    wd,
    acc,
    h,
    normed,
    side,
    lat,
    z_first_in,
    half_in,
    full_in,
    small_half_in,
    small_full_in,
    own_sum,
    z_in,
    final,
    send_sems,
    recv_sems,
    local_sems,
):
    e = lax.axis_index("expert")
    hid = lax.axis_index("hidden")
    y, xx, z, c = e // SIDE, e % SIDE, hid // 2, hid % 2
    other = 1 - c

    def at(dy=0, dx=0, dz=0, flip=False):
        core = other if flip else c
        return (
            ((y + dy) % SIDE) * SIDE + (xx + dx) % SIDE,
            ((z + dz) % SIDE) * 2 + core,
        )

    x_next, x_prev = at(dx=1), at(dx=3)
    y_next, y_prev = at(dy=1), at(dy=3)
    sibling = at(flip=True)

    keys = {}

    def sem_of(key):
        if key not in keys:
            keys[key] = len(keys)
            assert len(keys) <= N_SEMS
        return keys[key]

    pending = []

    def send(key, src, dst, device):
        i = sem_of(key)
        copy = pltpu.make_async_remote_copy(
            src_ref=src,
            dst_ref=dst,
            send_sem=send_sems.at[i],
            recv_sem=recv_sems.at[i],
            device_id=device,
            device_id_type=MESH,
        )
        copy.start()
        pending.append(copy)

    def arrived(key, landing):
        i = sem_of(key)
        pltpu.make_async_remote_copy(
            src_ref=landing,
            dst_ref=landing,
            send_sem=send_sems.at[i],
            recv_sem=recv_sems.at[i],
            device_id=sibling,
            device_id_type=MESH,
        ).wait_recv()

    def settle():
        for copy in pending:
            copy.wait_send()
        pending.clear()

    locals_ = []

    def local(src, dst):
        copy = pltpu.make_async_copy(src, dst, local_sems.at[len(locals_)])
        copy.start()
        locals_.append(copy)
        return copy

    big = (y, xx)
    small = (xx, y)
    big_next, big_prev = (y_next, x_next), (y_prev, x_prev)
    small_next, small_prev = (x_next, y_next), (x_prev, y_prev)
    STEP = (0, 3, 1, 2)

    def big_at(k, q):
        return (big[k] + STEP[q]) % SIDE

    def small_at(k, r):
        return (small[k] + STEP[r]) % SIDE

    def token_columns(k, half):
        return pl.ds(pl.multiple_of(half * (2 * PART) + k * PART, 128), PART)

    LOW, HIGH = pl.ds(0, HALF), pl.ds(HALF, HALF)

    barrier = pltpu.get_barrier_semaphore()
    partners = (x_next, x_prev, y_next, y_prev, at(dz=1), at(dz=2), at(dz=3), sibling)
    for partner in partners:
        pl.semaphore_signal(barrier, inc=1, device_id=partner, device_id_type=MESH)

    weight_loads = [local(gate, w.at[pl.ds(0, 2)]), local(up, w.at[pl.ds(2, 2)])]
    token_loads = [
        local(tokens.at[:, token_columns(k, half)], x.at[k, half, big[k], small[k]])
        for k in range(2)
        for half in range(2)
    ]

    chosen = routes[...]
    strength = route_weights[...]
    expert_row = lax.broadcasted_iota(jnp.int32, (N_EXPERTS, ROWS), 0)
    dense = jnp.zeros((N_EXPERTS, ROWS), jnp.float32)
    for j in range(TOP):
        dense = dense + jnp.where(expert_row == chosen[j : j + 1], strength[j : j + 1], 0.0)
    dense_high = dense.astype(jnp.bfloat16).astype(jnp.float32)
    packed = jnp.concatenate([dense_high, dense - dense_high], axis=1)
    packed = jnp.where(c == 0, packed[:QUARTER], packed[QUARTER:])

    head = latents[:, :KV_RANK].astype(jnp.float32)
    tail = latents[:, KV_RANK:].astype(jnp.float32)
    scale = lax.rsqrt(jnp.sum(head * head, axis=1, keepdims=True) / KV_RANK + 1e-06)
    lat_rows = latents.shape[0]
    row = lax.broadcasted_iota(jnp.int32, (lat_rows, 2 * LAT_PART - LAT), 0)
    marks = jnp.zeros(row.shape, jnp.float32)
    for i in range(lat_rows):
        marks = jnp.where(row == i, owners[i].astype(jnp.float32), marks)
    normed[0, :, :KV_RANK] = head * scale * kv_gain[...]
    normed[0, :, KV_RANK:] = jnp.concatenate([tail, marks], axis=1)

    pl.semaphore_wait(barrier, len(partners))

    def block(k, q, r):
        return x.at[k, c, big_at(k, q), small_at(k, r)]

    def send_block(key, k, q, r, device, rows=None):
        ref = block(k, q, r)
        if rows is not None:
            ref = ref.at[rows]
        send(key, ref, ref, device)

    def block_arrived(key, k, q, r, rows=None):
        ref = block(k, q, r)
        if rows is not None:
            ref = ref.at[rows]
        arrived(key, ref)

    def send_own(key, k, device):
        send(key, tokens.at[:, token_columns(k, c)], block(k, 0, 0), device)

    SIDE_LEFT, SIDE_RIGHT = pl.ds(0, SIDE_COLS // 2), pl.ds(SIDE_COLS // 2, SIDE_COLS // 2)

    def side_ref(dy=0, dx=0):
        return side.at[c, (y + dy) % SIDE, (xx + dx) % SIDE]

    def side_row(dy=0):
        return side.at[c, (y + dy) % SIDE]

    def side_one():
        arrived(("n",), normed.at[1])
        first = jnp.where(c == 0, normed[0], normed[1])
        second = jnp.where(c == 0, normed[1], normed[0])
        pair = jnp.concatenate([first, second], axis=0)
        pair = jnp.where(c == 0, pair[:, :LAT_PART], pair[:, LAT_PART:])
        side[c, y, xx] = jnp.concatenate([pair, packed], axis=1).astype(jnp.bfloat16)
        send(("g1p",), side_ref(), side_ref(), x_next)
        send(("g1m",), side_ref(), side_ref(), x_prev)

    def side_two():
        arrived(("g1p",), side_ref(dx=3))
        ref = side_ref(dx=3).at[:, SIDE_LEFT]
        send(("g2p",), ref, ref, x_next)
        arrived(("g1m",), side_ref(dx=1))
        ref = side_ref(dx=1).at[:, SIDE_RIGHT]
        send(("g2m",), ref, ref, x_prev)

    def side_three():
        arrived(("g2p",), side_ref(dx=2).at[:, SIDE_LEFT])
        arrived(("g2m",), side_ref(dx=2).at[:, SIDE_RIGHT])
        send(("g3p",), side_row(), side_row(), y_next)
        send(("g3m",), side_row(), side_row(), y_prev)

    def side_four():
        arrived(("g3p",), side_row(3))
        ref = side_row(3).at[:, :, SIDE_LEFT]
        send(("g4p",), ref, ref, y_next)
        arrived(("g3m",), side_row(1))
        ref = side_row(1).at[:, :, SIDE_RIGHT]
        send(("g4m",), ref, ref, y_prev)

    def side_done():
        arrived(("g4p",), side_row(2).at[:, :, SIDE_LEFT])
        arrived(("g4m",), side_row(2).at[:, :, SIDE_RIGHT])
        send(("gc",), side.at[c], side.at[c], sibling)

    def to_sibling(k, q, r):
        send(("c", k, q, r), block(k, q, r), block(k, q, r), sibling)

    def from_sibling(k, q, r):
        arrived(("c", k, q, r), x.at[k, other, big_at(k, q), small_at(k, r)])

    send(("n",), normed.at[0], normed.at[1], sibling)
    for k in (1, 0):
        send_own(("s1p", k), k, small_next[k])
        send_own(("s1m", k), k, small_prev[k])
    for k in (0, 1):
        send_own(("b1p", k, 0), k, big_next[k])
        send_own(("b1m", k, 0), k, big_prev[k])
    side_one()
    down_half = pl.ds(pl.multiple_of(c * (2 * PART), 128), 2 * PART)
    down_other = pl.ds(pl.multiple_of(other * (2 * PART), 128), 2 * PART)
    send(("wd",), down.at[:, :, down_other], wd.at[c], sibling)
    down_load = local(down.at[:, :, down_half], wd.at[c])
    acc[...] = jnp.zeros_like(acc)

    for k in (0, 1):
        block_arrived(("s1p", k), k, 0, 1)
        send_block(("s2p", k), k, 0, 1, small_next[k], LOW)
        block_arrived(("s1m", k), k, 0, 2)
        send_block(("s2m", k), k, 0, 2, small_prev[k], HIGH)
    for r in (1, 2):
        for k in (0, 1):
            send_block(("b1p", k, r), k, 0, r, big_next[k])
            send_block(("b1m", k, r), k, 0, r, big_prev[k])
            to_sibling(k, 0, r)
    for k in (0, 1):
        block_arrived(("s2p", k), k, 0, 3, LOW)
        block_arrived(("s2m", k), k, 0, 3, HIGH)
        send_block(("b1p", k, 3), k, 0, 3, big_next[k])
        send_block(("b1m", k, 3), k, 0, 3, big_prev[k])
        to_sibling(k, 0, 3)
    side_two()

    def long_step(r):
        for k in (0, 1):
            block_arrived(("b1p", k, r), k, 1, r)
            send_block(("b2p", k, r), k, 1, r, big_next[k], LOW)
            block_arrived(("b1m", k, r), k, 2, r)
            send_block(("b2m", k, r), k, 2, r, big_prev[k], HIGH)
            to_sibling(k, 1, r)
            to_sibling(k, 2, r)

    def far_step(r):
        for k in (0, 1):
            block_arrived(("b2p", k, r), k, 3, r, LOW)
            block_arrived(("b2m", k, r), k, 3, r, HIGH)
            to_sibling(k, 3, r)

    def multiply(k, half, blocks):
        start = half * (2 * PART) + k * PART
        places = [(big_at(k, q), small_at(k, r)) for q, r in blocks]

        left = jnp.concatenate([x[k, half, g, j] for g, j in places], axis=0)
        for n in range(4):
            right = w[n, pl.ds(pl.multiple_of(start, 128), PART), :]
            part = jnp.dot(left, right, preferred_element_type=jnp.float32)
            for i, (g, j) in enumerate(places):
                piece = part[i * ROWS : (i + 1) * ROWS]
                if k == 0:
                    acc[n, g, j] += piece
                else:
                    acc[n, j, g] += piece

    NEAR_ROW = ((0, 0), (0, 1), (0, 2), (0, 3))
    EARLY = ((1, 0), (1, 1), (2, 0), (2, 1))
    LATE = ((1, 2), (1, 3), (2, 2), (2, 3))
    FAR_ROW = ((3, 0), (3, 1), (3, 2), (3, 3))

    def rest(k, blocks):
        for q, r in blocks:
            if (q, r) != (0, 0):
                from_sibling(k, q, r)
        multiply(k, other, blocks)

    for copy in weight_loads + token_loads:
        copy.wait()
    long_step(0)
    for k in (0, 1):
        multiply(k, c, NEAR_ROW)
    side_three()
    long_step(1)
    for k in (0, 1):
        rest(k, NEAR_ROW)
    for k in (0, 1):
        multiply(k, c, EARLY)
    long_step(2)
    for k in (0, 1):
        rest(k, EARLY)
    side_four()
    long_step(3)
    far_step(0)
    for k in (0, 1):
        multiply(k, c, LATE)
    far_step(1)
    for k in (0, 1):
        rest(k, LATE)
    side_done()
    far_step(2)
    far_step(3)
    for k in (0, 1):
        multiply(k, c, FAR_ROW)
    for k in (0, 1):
        rest(k, FAR_ROW)

    expert = lax.broadcasted_iota(jnp.int32, (N_EXPERTS, 2 * UNITS), 0)
    column = lax.broadcasted_iota(jnp.int32, (N_EXPERTS, 2 * UNITS), 1)
    pick = (expert == 2 * e + column // UNITS).astype(jnp.bfloat16)
    arrived(("gc",), side.at[other])
    own_units = pl.ds(pl.multiple_of(c * (2 * UNITS), 128), 2 * UNITS)
    other_units = pl.ds(pl.multiple_of(other * (2 * UNITS), 128), 2 * UNITS)

    def activate(q):
        g = big_at(0, q)
        weights = []
        for j in range(SIDE):
            halves = [side[core, g, j, :, 3 * 128 :] for core in range(2)]
            both_parts = lax.dot_general(
                jnp.concatenate(halves, axis=0),
                pick,
                (((0,), (0,)), ((), ())),
                preferred_element_type=jnp.float32,
            )
            weights.append((both_parts[:ROWS] + both_parts[ROWS:])[None])
        weight = jnp.concatenate(weights, axis=0)
        for n in range(2):
            gate_val = acc[n, g]
            value = gate_val / (1.0 + jnp.exp(-gate_val)) * acc[2 + n, g]
            value = value * weight[:, :, n * UNITS : (n + 1) * UNITS]
            where = pl.ds(pl.multiple_of(c * (2 * UNITS) + n * UNITS, 128), UNITS)
            h[g, :, :, where] = value.astype(jnp.bfloat16)
        send(("h", q), h.at[g, :, :, own_units], h.at[g, :, :, own_units], sibling)

    for q in (3, 1, 2, 0):
        activate(q)
    settle()
    down_load.wait()
    arrived(("wd",), wd.at[other])
    def h_from_sibling(q):
        arrived(("h", q), h.at[big_at(0, q), :, :, other_units])


    FAR, NEXT, PREV, MINE = 0, 1, 2, 3

    def stage(k, slot):
        return x.at[k, 0, slot]

    def partial(k, q, first, width, slot, add=None):
        g = big_at(k, q)

        left = h[g] if k == 0 else h[:, g]
        left = left.reshape(SIDE * ROWS, 4 * UNITS)
        for start in range(first, first + width, 256):
            cols = pl.ds(start, 256)
            right = wd[:, :, :, pl.ds(k * PART + start, 256)].reshape(4 * UNITS, 256)
            part = jnp.dot(left, right, preferred_element_type=jnp.float32)
            part = part.reshape(SIDE, ROWS, 256)
            if add == "low":
                x[k, 0, slot, :, LOW, cols] = (
                    part[:, :HALF] + half_in[k, 0, :, :, cols].astype(jnp.float32)
                ).astype(jnp.bfloat16)
                x[k, 0, slot, :, HIGH, cols] = part[:, HALF:].astype(jnp.bfloat16)
            elif add == "high":
                x[k, 0, slot, :, LOW, cols] = part[:, :HALF].astype(jnp.bfloat16)
                x[k, 0, slot, :, HIGH, cols] = (
                    part[:, HALF:] + half_in[k, 1, :, :, cols].astype(jnp.float32)
                ).astype(jnp.bfloat16)
            else:
                if add == "both":
                    part = part + full_in[k, 0, :, :, cols].astype(jnp.float32)
                    part = part + full_in[k, 1, :, :, cols].astype(jnp.float32)
                x[k, 0, slot, :, :, cols] = part.astype(jnp.bfloat16)

    def gather_sum(ref, *others):
        total = ref[...].astype(jnp.float32)
        for one in others:
            total = total + one[...].astype(jnp.float32)
        ref[...] = total.astype(jnp.bfloat16)

    def own_of(d):
        return pl.ds(pl.multiple_of(FIRST + OWN * ((z + d) % SIDE), OWN), OWN)

    def piece(s):
        return own_of(0) if s == 2 else pl.ds(*SUBS[s])

    def z_first(k, i, slots, qs):
        for slot, q in zip(slots, qs):
            partial(k, q, FIRST, SIDE * OWN, slot)
        where = pl.ds(slots[0], len(slots))
        for d in (2, 1, 3):
            send(
                ("zq", k, i, d),
                x.at[k, 0, where, :, :, own_of(d)],
                z_first_in.at[k, d - 1, where],
                at(dz=d),
            )

    def z_first_sum(k, i, slots):
        where = pl.ds(slots[0], len(slots))
        for d in (1, 2, 3):
            arrived(("zq", k, i, d), z_first_in.at[k, d - 1, where])
        for slot in slots:
            gather_sum(
                x.at[k, 0, slot, :, :, own_of(0)],
                *[z_first_in.at[k, d, slot] for d in range(3)],
            )

    def back_far(k, s):
        if s < 2:
            partial(k, 3, *SUBS[s], FAR)
        cols = piece(s)
        send(
            ("rhp", k, s),
            stage(k, FAR).at[:, LOW, cols],
            half_in.at[k, 0, :, :, cols],
            big_next[k],
        )
        send(
            ("rhm", k, s),
            stage(k, FAR).at[:, HIGH, cols],
            half_in.at[k, 1, :, :, cols],
            big_prev[k],
        )

    def back_near(k, s):
        cols = piece(s)
        arrived(("rhp", k, s), half_in.at[k, 0, :, :, cols])
        if s < 2:
            partial(k, 2, *SUBS[s], NEXT, "low")
        else:
            gather_sum(stage(k, NEXT).at[:, LOW, cols], half_in.at[k, 0, :, :, cols])
        send(("rfp", k, s), stage(k, NEXT).at[:, :, cols], full_in.at[k, 0, :, :, cols], big_next[k])
        arrived(("rhm", k, s), half_in.at[k, 1, :, :, cols])
        if s < 2:
            partial(k, 1, *SUBS[s], PREV, "high")
        else:
            gather_sum(stage(k, PREV).at[:, HIGH, cols], half_in.at[k, 1, :, :, cols])
        send(("rfm", k, s), stage(k, PREV).at[:, :, cols], full_in.at[k, 1, :, :, cols], big_prev[k])

    def back_mine(k, s):
        cols = piece(s)
        arrived(("rfp", k, s), full_in.at[k, 0, :, :, cols])
        arrived(("rfm", k, s), full_in.at[k, 1, :, :, cols])
        if s < 2:
            partial(k, 0, *SUBS[s], MINE, "both")
        else:
            gather_sum(
                stage(k, MINE).at[:, :, cols],
                full_in.at[k, 0, :, :, cols],
                full_in.at[k, 1, :, :, cols],
            )
        far = stage(k, MINE).at[small_at(k, 3)]
        send(("thp", k, s), far.at[LOW, cols], small_half_in.at[k, 0, :, cols], small_next[k])
        send(("thm", k, s), far.at[HIGH, cols], small_half_in.at[k, 1, :, cols], small_prev[k])

    def back_small(k, s):
        cols = piece(s)
        arrived(("thp", k, s), small_half_in.at[k, 0, :, cols])
        block = stage(k, MINE).at[small_at(k, 2)]
        gather_sum(block.at[LOW, cols], small_half_in.at[k, 0, :, cols])
        send(("tfp", k, s), block.at[:, cols], small_full_in.at[k, 0, :, cols], small_next[k])
        arrived(("thm", k, s), small_half_in.at[k, 1, :, cols])
        block = stage(k, MINE).at[small_at(k, 1)]
        gather_sum(block.at[HIGH, cols], small_half_in.at[k, 1, :, cols])
        send(("tfm", k, s), block.at[:, cols], small_full_in.at[k, 1, :, cols], small_prev[k])

    def z_rows(d):
        return pl.ds(pl.multiple_of(((z + d) % SIDE) * QUARTER, QUARTER), QUARTER)

    def back_block(k, s):
        cols = piece(s)
        arrived(("tfp", k, s), small_full_in.at[k, 0, :, cols])
        arrived(("tfm", k, s), small_full_in.at[k, 1, :, cols])
        total = (
            x[k, 0, MINE, small[k], :, cols].astype(jnp.float32)
            + small_full_in[k, 0, :, cols].astype(jnp.float32)
            + small_full_in[k, 1, :, cols].astype(jnp.float32)
        ).astype(jnp.bfloat16)
        if s == 2:
            final[k, :, cols] = total
            mine = final.at[k, :, cols]
            for d in (2, 1, 3):
                send(("f", k, s, d), mine, mine, at(dz=d))
            return
        own_sum[k, :, cols] = total
        for d in (2, 1, 3):
            send(
                ("z", k, s, d),
                own_sum.at[k, z_rows(d), cols],
                z_in.at[k, d - 1, :, cols],
                at(dz=d),
            )

    def back_z(k, s):
        cols = piece(s)
        for d in (1, 2, 3):
            arrived(("z", k, s, d), z_in.at[k, d - 1, :, cols])
        total = own_sum[k, z_rows(0), cols].astype(jnp.float32)
        for d in (1, 2, 3):
            total = total + z_in[k, d - 1, :, cols].astype(jnp.float32)
        final[k, z_rows(0), cols] = total.astype(jnp.bfloat16)
        for d in (2, 1, 3):
            mine = final.at[k, z_rows(0), cols]
            send(("f", k, s, d), mine, mine, at(dz=d))

    last = []

    def columns_of(s):
        return (FIRST, SIDE * OWN) if s == 2 else SUBS[s]

    def back_out(k, s):
        for d in (1, 2, 3):
            if s == 2:
                landing = final.at[k, :, own_of(SIDE - d)]
            else:
                landing = final.at[k, z_rows(SIDE - d), piece(s)]
            arrived(("f", k, s, d), landing)
        first, width = columns_of(s)
        where = pl.ds(pl.multiple_of(c * (2 * PART) + k * PART + first, 128), width)
        src = final.at[k, :, pl.ds(first, width)]
        send(("o", k, s), src, out.at[:, where], sibling)
        last.append(local(src, out.at[:, where]))

    def back_sibling(k, s):
        first, width = columns_of(s)
        where = pl.ds(pl.multiple_of(other * (2 * PART) + k * PART + first, 128), width)
        arrived(("o", k, s), out.at[:, where])

    def lat_to_z():
        for d in (2, 1, 3):
            send(("lz", d), side.at[c, :, :, :, LAT_COLS], lat.at[c, :, :, z], at(dz=d))

    def lat_from_z():
        for d in (1, 2, 3):
            arrived(("lz", d), lat.at[c, :, :, (z + SIDE - d) % SIDE])
        lat[c, :, :, z] = side[c, :, :, :, LAT_COLS]
        send(("lc",), lat.at[c], lat.at[c], sibling)

    def place_latents():
        arrived(("lc",), lat.at[other])
        me = (e * (2 * SIDE) + hid).astype(jnp.float32)
        seek = lax.broadcasted_iota(jnp.int32, (8, LAT_PART), 1) == LAT_PART - 1
        seek = seek.astype(jnp.bfloat16)
        before = lax.broadcasted_iota(jnp.int32, (128, 128), 0)
        before = before < lax.broadcasted_iota(jnp.int32, (128, 128), 1)
        before = before.astype(jnp.bfloat16)
        slot = lax.broadcasted_iota(jnp.int32, (SLOTS, 128), 0).astype(jnp.float32)
        taken = jnp.zeros((8, 1), jnp.float32)
        sums = [jnp.zeros((SLOTS, LAT_PART), jnp.float32) for _ in range(2)]
        for yy in range(SIDE):
            for pair_of in range(2):
                rows = [
                    lat[core, yy, 2 * pair_of : 2 * pair_of + 2].reshape(128, LAT_PART)
                    for core in range(2)
                ]
                owner = lax.dot_general(
                    seek, rows[1], (((1,), (1,)), ((), ())), preferred_element_type=jnp.float32
                )
                mine = (owner == me).astype(jnp.float32)
                earlier = taken + jnp.dot(
                    mine.astype(jnp.bfloat16), before, preferred_element_type=jnp.float32
                )
                taken = taken + jnp.sum(mine, axis=1, keepdims=True)
                place = jnp.where(earlier[:1] == slot, mine[:1], 0.0).astype(jnp.bfloat16)
                for core in range(2):
                    sums[core] = sums[core] + jnp.dot(
                        place, rows[core], preferred_element_type=jnp.float32
                    )
        cache[:, :LAT_PART] = sums[0].astype(jnp.bfloat16)
        cache[:, LAT_PART:] = sums[1][:, : LAT - LAT_PART].astype(jnp.bfloat16)

    both = (0, 1)

    def do(step, s):
        for k in both:
            step(k, s)

    h_from_sibling(3)
    back_far(0, 0)
    for q in (1, 2, 0):
        h_from_sibling(q)
    back_far(1, 0)
    for k in both:
        z_first(k, 0, (FAR,), (3,))
    do(back_far, 1)
    for k in both:
        z_first(k, 1, (NEXT, PREV), (2, 1))
    do(back_near, 0)
    for k in both:
        z_first(k, 2, (MINE,), (0,))
    lat_to_z()
    do(back_near, 1)
    for k in both:
        z_first_sum(k, 0, (FAR,))
    do(back_far, 2)
    do(back_mine, 0)
    for k in both:
        z_first_sum(k, 1, (NEXT, PREV))
    do(back_near, 2)
    do(back_mine, 1)
    do(back_small, 0)
    for k in both:
        z_first_sum(k, 2, (MINE,))
    do(back_mine, 2)
    do(back_small, 1)
    do(back_block, 0)
    do(back_small, 2)
    lat_from_z()
    do(back_block, 1)
    do(back_z, 0)
    do(back_block, 2)
    place_latents()
    do(back_z, 1)
    do(back_out, 0)
    do(back_out, 2)
    do(back_out, 1)
    for s in (0, 2, 1):
        do(back_sibling, s)
    for copy in last:
        copy.wait()
    settle()


def layer(tokens, routes, route_weights, gate, up, down, latents, kv_gain, owners):
    bf16 = jnp.bfloat16
    anywhere = pl.BlockSpec(memory_space=pl.ANY)
    vmem = pl.BlockSpec(memory_space=pltpu.VMEM)
    smem = pl.BlockSpec(memory_space=pltpu.SMEM)
    return pl.pallas_call(
        moe_kernel,
        out_shape=(
            jax.ShapeDtypeStruct((ROWS, WIDE), bf16),
            jax.ShapeDtypeStruct((SLOTS, LAT), bf16),
        ),
        in_specs=[anywhere, vmem, vmem, anywhere, anywhere, anywhere, vmem, vmem, smem],
        out_specs=(anywhere, vmem),
        scratch_shapes=[
            pltpu.VMEM((2, 2, SIDE, SIDE, ROWS, PART), bf16),
            pltpu.VMEM((4, WIDE, UNITS), bf16),
            pltpu.VMEM((2, 2, UNITS, 2 * PART), bf16),
            pltpu.VMEM((4, SIDE, SIDE, ROWS, UNITS), jnp.float32),
            pltpu.VMEM((SIDE, SIDE, ROWS, 4 * UNITS), bf16),
            pltpu.VMEM((2, 8, 2 * LAT_PART), jnp.float32),
            pltpu.VMEM((2, SIDE, SIDE, QUARTER, SIDE_COLS), bf16),
            pltpu.VMEM((2, SIDE, SIDE, SIDE, QUARTER, LAT_PART), bf16),
            pltpu.VMEM((2, 3, SIDE, SIDE, ROWS, OWN), bf16),
            pltpu.VMEM((2, 2, SIDE, HALF, PART), bf16),
            pltpu.VMEM((2, 2, SIDE, ROWS, PART), bf16),
            pltpu.VMEM((2, 2, HALF, PART), bf16),
            pltpu.VMEM((2, 2, ROWS, PART), bf16),
            pltpu.VMEM((2, ROWS, PART), bf16),
            pltpu.VMEM((2, 3, QUARTER, PART), bf16),
            pltpu.VMEM((2, ROWS, PART), bf16),
            pltpu.SemaphoreType.DMA((N_SEMS,)),
            pltpu.SemaphoreType.DMA((N_SEMS,)),
            pltpu.SemaphoreType.DMA((16,)),
        ],
        compiler_params=pltpu.CompilerParams(
            collective_id=0, has_side_effects=True, vmem_limit_bytes=60 << 20
        ),
        cost_estimate=pl.CostEstimate(
            flops=2 * 3 * 1024 * WIDE * 512, bytes_accessed=24 << 20, transcendentals=1 << 19
        ),
        name="moe",
    )(tokens, routes, route_weights, gate, up, down, latents, kv_gain, owners)


def hand_over_kernel(moe_in, cache_in, moe_out, cache_out):
    moe_out[...] = moe_in[...]
    cache_out[...] = cache_in[...]


def hand_over(moe_out, cache):
    vmem = pl.BlockSpec(memory_space=pltpu.VMEM)
    return pl.pallas_call(
        hand_over_kernel,
        out_shape=tuple(jax.ShapeDtypeStruct(a.shape, a.dtype) for a in (moe_out, cache)),
        in_specs=[vmem, vmem],
        out_specs=(vmem, vmem),
        name="hand_over",
    )(moe_out, cache)


def body(tokens, routes, route_weights, gate_proj, up_proj, down_proj, latents, kv_gain, owners):
    moe_out, cache = layer(
        tokens,
        routes.T,
        route_weights.T,
        gate_proj,
        up_proj,
        down_proj,
        latents,
        kv_gain.reshape(1, KV_RANK),
        owners,
    )
    return hand_over(moe_out, cache)


def solution(mesh):
    return jax.shard_map(
        body,
        mesh=mesh,
        in_specs=(
            P("expert", None),
            P("expert", None),
            P("expert", None),
            P("expert", None, "hidden"),
            P("expert", None, "hidden"),
            P("expert", "hidden", None),
            P(("expert", "hidden"), None),
            P(),
            P(("expert", "hidden")),
        ),
        out_specs=(P("expert", None), P(("expert", "hidden"), None)),
        check_vma=False,
    )
```
